32 devices in a mesh: groups: 2 (over x), col: 16 (over z, y, core).
Axes of the slice: x: 2, y: 2, z: 4, core: 2. Of those that a mesh axis runs over, the one named last changes fastest.
Arguments:
- probes: int32 [32, 16384], P(None, ('groups', 'col')), parts along dimension 1, may hold values from 0 to 1
- diag_tiles: float32 [16384, 512], P(('groups', 'col')), parts along dimension 0, as said below
- forward_tiles: float32 [32, 5, 512, 512], P(('groups', 'col')), parts along dimension 0, as said below
- tile_columns: int32 [32, 5], P(('groups', 'col')), parts along dimension 0, may hold values from 0 to 15, as said below
Outputs:
- next_basis: float32 [32, 16384], P(None, ('groups', 'col')), parts along dimension 1
- lanczos_blocks: float32 [8, 32, 32], P('groups'), parts along dimension 0
The draws below stay inside these ranges and needn't reach their ends.
There are 2 independent parts, one for each index of `groups`. The reference program is written for one: setup_inputs(seed, part) draws one part's arguments, and reference() takes and returns one part's arrays. A program takes and returns all parts, laid end to end along the dimension named above; each array names one. Nothing has to cross between parts.
Inputs may be any that keep to these rules, and one draw needn't show every extreme that they name: `tile_columns`: the 5 entries of row block r are distinct and each is (r + d) mod 16 for some d from 1 to 7. `diag_tiles`: each diagonal tile is symmetric. `forward_tiles`: entries of any size and sign.
All inputs are finite; a program needn't handle non-finite values.
Results may differ from the reference program's by a relative error of at most 0.0003.
Values sent between devices are 32-bit elements; how exact they have to be, the bound alone decides.
No kernel may reach another device: no remote copies, remote signals or barrier semaphores. Data moves between devices by JAX's collectives and lax.ppermute only.
A program may use at most 64 MiB of HBM per device.

```python
import math
import jax
import jax.numpy as jnp
from jax import lax

BLK = 512
P_SIZE = 32
E = 5
REACH = 7
BLOCKS = 16
ORDER = 8192


def row_scales(key, lowest, highest, exponent):
    scale_key = jax.random.fold_in(key, 7)
    random_scale = jnp.exp(jax.random.uniform(scale_key, (ORDER,), jnp.float32, math.log(lowest), math.log(highest)))
    position = jnp.arange(ORDER, dtype=jnp.float32) / (ORDER - 1)
    return random_scale * (1.0 + 2.0 * position) ** exponent


def column_blocks(key):
    row_keys = jax.random.split(jax.random.fold_in(key, 5), BLOCKS)
    shuffles = jax.vmap(lambda single: jax.random.permutation(single, REACH))(row_keys)
    offsets = shuffles[:, :E].astype(jnp.int32) + 1
    return ((jnp.arange(BLOCKS, dtype=jnp.int32)[:, None] + offsets) % BLOCKS).astype(jnp.int32)


def draw_tile_columns(key, part):
    return column_blocks(key)


def draw_diag_tiles(key, part):
    scales = row_scales(key, 0.3, 0.9, 0.5)
    key = jax.random.fold_in(key, 21)
    spread = 1.0 / math.sqrt(BLK * (2 * E + 1))
    gaussian = jnp.clip(jax.random.normal(key, (BLOCKS, BLK, BLK), jnp.float32), -5.0, 5.0)
    symmetric = (gaussian + jnp.transpose(gaussian, (0, 2, 1))) * (spread / math.sqrt(2.0))
    center = 3.0 * jnp.eye(BLK, dtype=jnp.float32)[None, :, :] + symmetric
    blocked = scales.reshape(BLOCKS, BLK)
    values = blocked[:, :, None] * center * blocked[:, None, :]
    return values.reshape(ORDER, BLK).astype(jnp.float32)


def draw_forward_tiles(key, part):
    scales = row_scales(key, 0.3, 0.9, 0.5)
    columns = column_blocks(key)
    key = jax.random.fold_in(key, 33)
    spread = 1.0 / math.sqrt(BLK * (2 * E + 1))
    blocked = scales.reshape(BLOCKS, BLK)
    column_scale = blocked[columns]
    gaussian = jnp.clip(jax.random.normal(key, (BLOCKS, E, BLK, BLK), jnp.float32), -5.0, 5.0) * spread
    values = blocked[:, None, :, None] * gaussian * column_scale[:, :, None, :]
    return values.astype(jnp.float32)


def set_ends(array, key, least, largest):
    place = [jax.random.randint(jax.random.fold_in(key, axis), (), 0, length) for axis, length in enumerate(array.shape)]
    main_axis = array.shape.index(max(array.shape))
    next_to = place[:main_axis] + [(place[main_axis] + 1) % array.shape[main_axis]] + place[main_axis + 1:]
    return array.at[tuple(place)].set(least).at[tuple(next_to)].set(largest)


def setup_inputs(seed: int = 0, part: int = 0) -> dict:
    key_of = jax.random.split(jax.random.key(seed), 5)
    part_splits = jax.random.split(jax.random.fold_in(key_of[4], part), 5)
    probes = set_ends(jax.random.randint(part_splits[0], (P_SIZE, ORDER), 0, 2), jax.random.fold_in(part_splits[0], 1), 0, 1).astype(jnp.int32)
    diag_tiles = draw_diag_tiles(jax.random.fold_in(jax.random.fold_in(key_of[4], part), 71), part)
    forward_tiles = draw_forward_tiles(jax.random.fold_in(jax.random.fold_in(key_of[4], part), 71), part)
    tile_columns = draw_tile_columns(jax.random.fold_in(jax.random.fold_in(key_of[4], part), 71), part)
    return {"probes": probes, "diag_tiles": diag_tiles, "forward_tiles": forward_tiles, "tile_columns": tile_columns}


precise = lax.Precision.HIGHEST

def gram_of(vectors):
    return jnp.einsum('pi,qi->pq', vectors, vectors, precision=precise)

def orthonormal(vectors, matrix):
    factor = jnp.linalg.cholesky(matrix)
    return (jax.scipy.linalg.solve_triangular(factor, vectors, lower=True), factor)

def apply_kernel(vectors, diag_tiles, forward_tiles, tile_columns):
    blocked = vectors.reshape(P_SIZE, BLOCKS, BLK)
    diagonal = diag_tiles.reshape(BLOCKS, BLK, BLK)
    result = jnp.einsum('pri,rij->prj', blocked, diagonal, precision=precise)
    needed = blocked[:, tile_columns, :]
    result = result + jnp.einsum('prej,reij->pri', needed, forward_tiles, precision=precise)
    returned = jnp.einsum('pri,reij->prej', blocked, forward_tiles, precision=precise)
    result = result.at[:, tile_columns, :].add(returned)
    return result.reshape(P_SIZE, ORDER)

def reference(probes, diag_tiles, forward_tiles, tile_columns):
    signs = 2.0 * probes.astype(jnp.float32) - 1.0
    first_basis = orthonormal(signs, gram_of(signs))[0]
    image = apply_kernel(first_basis, diag_tiles, forward_tiles, tile_columns)
    alpha_one = jnp.einsum('pi,qi->pq', image, first_basis, precision=precise)
    remainder = image - jnp.einsum('pq,qi->pi', alpha_one, first_basis, precision=precise)
    second_basis, beta_one = orthonormal(remainder, gram_of(remainder))
    image = apply_kernel(second_basis, diag_tiles, forward_tiles, tile_columns)
    image = image - jnp.einsum('qp,qi->pi', beta_one, first_basis, precision=precise)
    alpha_two = jnp.einsum('pi,qi->pq', image, second_basis, precision=precise)
    remainder = image - jnp.einsum('pq,qi->pi', alpha_two, second_basis, precision=precise)
    next_basis, beta_two = orthonormal(remainder, gram_of(remainder))
    return (next_basis, jnp.stack([alpha_one, beta_one, alpha_two, beta_two]))
```

```python
import jax
import jax.numpy as jnp
from jax import lax
from jax.sharding import PartitionSpec as P

REACH = 7


precise = lax.Precision.HIGHEST


def from_behind(block, axis, distance):
    devices = range(lax.axis_size(axis))
    route = [((i - distance) % len(devices), i) for i in devices]
    return lax.ppermute(block, axis, route)


def total(block, axis):
    devices = lax.axis_size(axis)
    if devices & (devices - 1):
        return lax.psum(block, axis)
    stride = 1
    while stride < devices:
        block = block + lax.ppermute(block, axis, [(i ^ stride, i) for i in range(devices)])
        stride *= 2
    return block


def gram_of(vectors):
    return jnp.einsum("pi,qi->pq", vectors, vectors, precision=precise)


def orthonormal(vectors, matrix):
    factor = jnp.linalg.cholesky(matrix)
    return (jax.scipy.linalg.solve_triangular(factor, vectors, lower=True), factor)


def apply_kernel(vectors, diagonal, forward, chooser):
    product = jnp.einsum("pi,ij->pj", vectors, diagonal, precision=precise)
    nearby = []
    for offset in range(1, REACH + 1):
        nearby.append(from_behind(vectors, "col", -offset))
    needed = jnp.einsum("ed,dpj->pej", chooser, jnp.stack(nearby), precision=precise)
    product = product + jnp.einsum("pej,eij->pi", needed, forward, precision=precise)
    outgoing = jnp.einsum("pi,eij->epj", vectors, forward, precision=precise)
    routed = jnp.einsum("ed,epj->dpj", chooser, outgoing, precision=precise)
    for offset in range(1, REACH + 1):
        product = product + from_behind(routed[offset - 1], "col", offset)
    return product


def project(image, basis):
    alpha = total(jnp.einsum("pi,qi->pq", image, basis, precision=precise), "col")
    remainder = image - jnp.einsum("pq,qi->pi", alpha, basis, precision=precise)
    matrix = total(gram_of(remainder), "col")
    return (alpha, remainder, matrix)


def body(probes, diag_tiles, forward_tiles, tile_columns):
    forward = forward_tiles[0]
    columns = tile_columns[0]
    cycle_size = lax.axis_size("col")
    position = lax.axis_index("col")
    distance = (columns - position) % cycle_size
    chooser = (distance[:, None] == jnp.arange(1, REACH + 1, dtype=jnp.int32)[None, :]).astype(
        jnp.float32
    )
    signs = 2.0 * probes.astype(jnp.float32) - 1.0
    first_basis = orthonormal(signs, total(gram_of(signs), "col"))[0]
    image = apply_kernel(first_basis, diag_tiles, forward, chooser)
    alpha_one, remainder, matrix = project(image, first_basis)
    second_basis, beta_one = orthonormal(remainder, matrix)
    image = apply_kernel(second_basis, diag_tiles, forward, chooser)
    image = image - jnp.einsum("qp,qi->pi", beta_one, first_basis, precision=precise)
    alpha_two, remainder, matrix = project(image, second_basis)
    next_basis, beta_two = orthonormal(remainder, matrix)
    return (next_basis, jnp.stack([alpha_one, beta_one, alpha_two, beta_two]))


def solution(mesh):
    placed = (
        P(None, ("groups", "col")),
        P(("groups", "col"), None),
        P(("groups", "col"), None, None, None),
        P(("groups", "col"), None),
    )
    return jax.shard_map(
        body,
        mesh=mesh,
        in_specs=placed,
        out_specs=(P(None, ("groups", "col")), P("groups", None, None)),
        check_vma=False,
    )
```

```python
import functools

import jax
import jax.numpy as jnp
from jax import lax
from jax.experimental import pallas as pl
from jax.experimental.pallas import tpu as pltpu
from jax.sharding import PartitionSpec as P

REACH = 7
SCALE = 0.0078125
SIDE = 128

precise = lax.Precision.HIGHEST
roomy = pltpu.CompilerParams(vmem_limit_bytes=40 * 1024 * 1024)
in_vmem = pl.BlockSpec(memory_space=pltpu.VMEM)
in_smem = pl.BlockSpec(memory_space=pltpu.SMEM)


def struct(*shape):
    return jax.ShapeDtypeStruct(shape, jnp.float32)


def mm(left, right):
    return lax.dot_general(
        left, right, (((1,), (0,)), ((), ())), precision=precise, preferred_element_type=jnp.float32
    )


def mm_t(left, right):
    return lax.dot_general(
        left, right, (((1,), (1,)), ((), ())), precision=precise, preferred_element_type=jnp.float32
    )


def halves(block):
    high = block.astype(jnp.bfloat16)
    return high, (block - high.astype(jnp.float32)).astype(jnp.bfloat16)


def split_product(vectors, matrix, side):
    dims = (((1,), (side,)), ((), ()))
    dot = functools.partial(lax.dot_general, dimension_numbers=dims, preferred_element_type=jnp.float32)
    high, low = vectors
    matrix_high, matrix_low = halves(matrix)
    if low is None:
        return dot(high, matrix_high) + dot(high, matrix_low)
    rows = high.shape[0]
    both = dot(jnp.concatenate([high, low], axis=0), matrix_high)
    return both[:rows] + both[rows:] + dot(high, matrix_low)


def parts_of(block, exact):
    if exact:
        return block.astype(jnp.bfloat16), None
    return halves(block)


def factor(matrix):
    size = matrix.shape[0]
    step = 8
    strips = size // step
    lane = lax.broadcasted_iota(jnp.int32, (step, size), 1)
    rows = [lax.broadcasted_iota(jnp.int32, (step, size), 0) + step * s for s in range(strips)]
    columns = [
        [jnp.broadcast_to(matrix[step * s : step * s + step, j : j + 1], (step, size)) for s in range(strips)]
        for j in range(size)
    ]
    inverse = [jnp.where(lane == rows[s], 1.0, 0.0) for s in range(strips)]
    lower = [jnp.zeros((step, size), jnp.float32) for _ in range(strips)]
    for k in range(size):
        home, at = divmod(k, step)
        pivot = jnp.broadcast_to(columns[k][home][at : at + 1, :], (step, size))
        root = lax.rsqrt(pivot)
        root = root * (1.5 - 0.5 * (pivot * root) * root)
        scaled = [None] * strips
        for s in range(home, strips):
            scaled[s] = columns[k][s] * root
            if s == home:
                scaled[s] = jnp.where(rows[s] >= k, scaled[s], 0.0)
            lower[s] = jnp.where(lane == k, scaled[s], lower[s])
        for j in range(k + 1, size):
            place, inside = divmod(j, step)
            weight = jnp.broadcast_to(scaled[place][inside : inside + 1, :], (step, size))
            for s in range(place, strips):
                columns[j][s] = columns[j][s] - scaled[s] * weight
        done = jnp.broadcast_to(inverse[home][at : at + 1, :], (step, size)) * root
        for s in range(home, strips):
            if s == home:
                inverse[s] = jnp.where(rows[s] == k, done, inverse[s] - jnp.where(rows[s] > k, scaled[s], 0.0) * done)
            else:
                inverse[s] = inverse[s] - scaled[s] * done
    return jnp.concatenate(lower, axis=0), jnp.concatenate(inverse, axis=0)


def begin_kernel(probes_ref, diagonal_ref, message_ref):
    signs = (2 * probes_ref[...] - 1).astype(jnp.float32) * SCALE
    rows, order = signs.shape
    message_ref[:, :order] = signs
    message_ref[:, order : order + rows] = mm_t(signs, signs)
    square = lax.broadcasted_iota(jnp.int32, (SIDE, SIDE), 0) == lax.broadcasted_iota(jnp.int32, (SIDE, SIDE), 1)
    trace = jnp.zeros((1, SIDE), jnp.float32)
    for start in range(0, order, SIDE):
        tile = diagonal_ref[start : start + SIDE, start : start + SIDE]
        trace += jnp.sum(jnp.where(square, tile, 0.0) * (1.0 / order), axis=0, keepdims=True)
    trace = jnp.sum(trace, axis=1, keepdims=True)
    message_ref[:, order + rows :] = jnp.broadcast_to(trace, (rows, SIDE - rows))


def outgoing_kernel(exact, distance_ref, vectors_ref, forward_ref, own_ref, other_ref):
    order = forward_ref.shape[1]
    vectors = parts_of(vectors_ref[:, :order], exact)
    own_ref[...] = jnp.zeros_like(own_ref)
    other_ref[...] = jnp.zeros_like(other_ref)

    def step(e, _):
        product = split_product(vectors, forward_ref[e], 0)
        distance = distance_ref[e]
        half = distance >> 1

        @pl.when((distance & 1) == 0)
        def _():
            own_ref[half - 1] = product

        @pl.when((distance & 1) == 1)
        def _():
            other_ref[half] = product

        return 0

    lax.fori_loop(0, forward_ref.shape[0], step, 0)


def incoming_kernel(
    exact, distance_ref, vectors_ref, far_ref, middle_ref, odd_ref, forward_ref, diagonal_ref, trace_ref, image_ref, table
):
    order = forward_ref.shape[1]
    rows = vectors_ref.shape[0]
    table[0] = far_ref[:, :order]
    table[1] = middle_ref[:, :order]
    table[2] = far_ref[:, order : 2 * order]
    for j in range(4):
        table[3 + j] = odd_ref[j]
    vectors = vectors_ref[:, :order]
    trace = trace_ref[0:1, order + rows : order + rows + 1]
    line = lax.broadcasted_iota(jnp.int32, (order, order), 0) == lax.broadcasted_iota(jnp.int32, (order, order), 1)
    rest = diagonal_ref[...] - jnp.where(line, trace, 0.0)
    image_ref[...] = split_product(parts_of(vectors, exact), rest, 0)

    def step(e, _):
        distance = distance_ref[e]
        half = distance >> 1
        slot = jnp.where((distance & 1) == 0, half - 1, half + 3)
        image_ref[...] += split_product(parts_of(table[slot], exact), forward_ref[e], 1)
        return 0

    lax.fori_loop(0, forward_ref.shape[0], step, 0)


def first_kernel(devices, start_ref, image_ref, total_ref, sums_ref, message_ref):
    rows, order = image_ref.shape
    signs = start_ref[:, :order]
    shift = start_ref[0:1, order + rows : order + rows + 1] - sums_ref[0:1, rows : rows + 1] * (1.0 / devices)
    image = image_ref[...] + total_ref[...] + shift * signs
    message_ref[:, :order] = image
    both = mm_t(jnp.concatenate([signs, image], axis=0), image)
    message_ref[:, order : order + rows] = both[:rows]
    message_ref[:, order + rows : order + 2 * rows] = both[rows:]
    message_ref[:, order + 2 * rows :] = jnp.zeros((rows, SIDE - 2 * rows), jnp.float32)


def root_kernel(sums_ref, inverse_ref):
    rows = sums_ref.shape[0]
    inverse_ref[...] = factor(sums_ref[:, :rows])[1]


def coefficient_kernel(root_ref, sums_ref, out_ref):
    rows = root_ref.shape[0]
    root = root_ref[...]
    alpha = mm_t(mm(root, sums_ref[:, :rows]), root)
    gram = mm_t(mm(root, sums_ref[:, rows : 2 * rows]), root) - mm_t(alpha, alpha)
    beta, inverse = factor(gram)
    scaled = mm(inverse, root)
    back = mm(mm(inverse, alpha), root)
    link = lax.dot_general(
        beta, root, (((0,), (0,)), ((), ())), precision=precise, preferred_element_type=jnp.float32
    )
    out_ref[0] = scaled
    out_ref[1] = back
    out_ref[2] = link
    out_ref[3] = alpha
    out_ref[4] = beta


def second_kernel(
    devices, start_ref, message_ref, image_ref, total_ref, small_ref, sums_ref, basis_ref, result_ref, share_ref
):
    rows, order = image_ref.shape
    signs = start_ref[:, :order]
    first = message_ref[:, :order]
    mean = sums_ref[0:1, rows : rows + 1] * (1.0 / devices)
    shift = start_ref[0:1, order + rows : order + rows + 1] - mean
    image = image_ref[...] + total_ref[...] + shift * first
    scaled, back, link, alpha, beta = (small_ref[j] for j in range(5))
    basis = mm(scaled, first) - mm(back, signs)
    result = mm(scaled, image) - mm(back, first) - mm(link, signs)
    basis_ref[...] = basis
    result_ref[...] = result
    both = mm_t(jnp.concatenate([basis, result], axis=0), result)
    line = lax.broadcasted_iota(jnp.int32, (rows, rows), 0)
    lane = lax.broadcasted_iota(jnp.int32, (rows, rows), 1)
    part = 1.0 / devices
    share_ref[:, :rows] = both[:rows]
    share_ref[:, rows : 2 * rows] = both[rows:]
    share_ref[:, 2 * rows : 3 * rows] = (alpha + jnp.where(line == lane, mean, 0.0)) * part
    share_ref[:, 3 * rows :] = jnp.where(lane > line, mean, beta) * part


def last_kernel(share_ref, basis_ref, result_ref, next_ref, blocks_ref):
    rows = share_ref.shape[0]
    line = lax.broadcasted_iota(jnp.int32, (rows, rows), 0)
    lane = lax.broadcasted_iota(jnp.int32, (rows, rows), 1)
    alpha = share_ref[:, :rows]
    mean = share_ref[0:1, 4 * rows - 1 : 4 * rows]
    gram = share_ref[:, rows : 2 * rows] - mm_t(alpha, alpha)
    beta, inverse = factor(gram)
    next_ref[...] = mm(inverse, result_ref[...] - mm(alpha, basis_ref[...]))
    blocks_ref[0] = share_ref[:, 2 * rows : 3 * rows]
    blocks_ref[1] = jnp.where(lane > line, 0.0, share_ref[:, 3 * rows :])
    blocks_ref[2] = alpha + jnp.where(line == lane, mean, 0.0)
    blocks_ref[3] = beta


def call(kernel, out_shape, args, smem=0, scratch=(), flops=0):
    outs = in_vmem if not isinstance(out_shape, tuple) else (in_vmem,) * len(out_shape)
    return pl.pallas_call(
        kernel,
        out_shape=out_shape,
        in_specs=[in_smem] * smem + [in_vmem] * (len(args) - smem),
        out_specs=outs,
        scratch_shapes=list(scratch),
        compiler_params=roomy,
        cost_estimate=pl.CostEstimate(flops=flops, bytes_accessed=4 * sum(a.size for a in args), transcendentals=0),
    )(*args)


def body(probes, diagonal, forward_tiles, tile_columns):
    forward = forward_tiles[0]
    rows, order = probes.shape
    devices = lax.axis_size("col")
    position = lax.axis_index("col")
    core = position & 1
    distance = (tile_columns[0] - position) % devices

    def arriving(block, hops):
        return lax.ppermute(block, "col", [((i - hops) % devices, i) for i in range(devices)])

    def swapped(block, bits=1):
        return lax.ppermute(block, "col", [(i ^ bits, i) for i in range(devices)])

    def spread(message):
        block, sums = message[:, :order], message[:, order:]
        farthest = arriving(message, -8)
        middle = arriving(message, -4)
        sums = sums + farthest[:, order:]
        far = arriving(jnp.concatenate([block, middle[:, :order], sums], axis=1), -2)
        sums = sums + far[:, 2 * order :]
        near, third = far[:, :order], far[:, order : 2 * order]
        ahead = [block, near, middle[:, :order], third, farthest[:, :order]]
        odd = swapped(jnp.stack([jnp.where(core == 0, ahead[j + 1], ahead[j]) for j in range(4)]))
        sums = sums + arriving(sums, -4)
        hops = 16
        while hops < devices:
            sums = sums + arriving(sums, -hops)
            hops *= 2
        return far, middle, odd, sums + swapped(sums)

    def gathered(own, other):
        other = swapped(other)
        ahead = [jnp.where(core == 0, 0.0, other[0])]
        for j in range(1, 4):
            ahead.append(own[j - 1] + jnp.where(core == 0, other[j - 1], other[j]))
        ahead.append(jnp.where(core == 0, other[3], 0.0))
        near = arriving(jnp.stack([ahead[1], ahead[3]]), 2)
        farthest = arriving(ahead[4], 8)
        middle = arriving(ahead[2] + near[1], 4)
        return ahead[0] + near[0] + middle + farthest

    def products(message, exact):
        return call(
            functools.partial(outgoing_kernel, exact),
            (struct(3, rows, order), struct(4, rows, order)),
            (distance, message, forward),
            smem=1,
            flops=2 * rows * forward.size * 3,
        )

    def images(message, near, exact, start):
        far, middle, odd = near
        return call(
            functools.partial(incoming_kernel, exact),
            struct(rows, order),
            (distance, message, far, middle, odd, forward, diagonal, start),
            smem=1,
            scratch=(pltpu.VMEM((REACH, rows, order), jnp.float32),),
            flops=2 * rows * forward.size * 3,
        )

    start = call(begin_kernel, struct(rows, order + SIDE), (probes, diagonal))
    far, middle, odd, start_sums = spread(start)
    own, other = products(start, True)
    image = images(start, (far, middle, odd), True, start)
    total = gathered(own, other)
    message = call(functools.partial(first_kernel, devices), struct(rows, order + SIDE), (start, image, total, start_sums))

    root = call(root_kernel, struct(rows, rows), (start_sums,))
    far, middle, odd, sums = spread(message)
    own, other = products(message, False)
    image = images(message, (far, middle, odd), False, start)
    total = gathered(own, other)
    small = call(coefficient_kernel, struct(5, rows, rows), (root, sums))
    basis, result, share = call(
        functools.partial(second_kernel, devices),
        (struct(rows, order), struct(rows, order), struct(rows, SIDE)),
        (start, message, image, total, small, start_sums),
    )
    bits = 1
    while bits < devices:
        if bits >= 4 and 4 * bits <= devices:
            one, two, three = (swapped(share, bits * j) for j in (1, 2, 3))
            share = (share + one) + (two + three)
            bits *= 4
        else:
            share = share + swapped(share, bits)
            bits *= 2
    return call(last_kernel, (struct(rows, order), struct(4, rows, rows)), (share, basis, result))


def solution(mesh):
    placed = (
        P(None, ("groups", "col")),
        P(("groups", "col"), None),
        P(("groups", "col"), None, None, None),
        P(("groups", "col"), None),
    )
    return jax.shard_map(
        body,
        mesh=mesh,
        in_specs=placed,
        out_specs=(P(None, ("groups", "col")), P("groups", None, None)),
        check_vma=False,
    )
```

```python
import functools

import jax
import jax.numpy as jnp
from jax import lax
from jax.experimental import pallas as pl
from jax.experimental.pallas import tpu as pltpu
from jax.sharding import PartitionSpec as P

SCALE = 0.0078125
SIDE = 128
PAD = 8

precise = lax.Precision.HIGHEST
in_vmem = pl.BlockSpec(memory_space=pltpu.VMEM)
in_hbm = pl.BlockSpec(memory_space=pltpu.HBM)
in_smem = pl.BlockSpec(memory_space=pltpu.SMEM)


def struct(*shape):
    return pltpu.VMEM(shape, jnp.float32)


def mm(left, right):
    return lax.dot_general(
        left, right, (((1,), (0,)), ((), ())), precision=precise, preferred_element_type=jnp.float32
    )


def mm_t(left, right):
    return lax.dot_general(
        left, right, (((1,), (1,)), ((), ())), precision=precise, preferred_element_type=jnp.float32
    )


def halves(block):
    high = block.astype(jnp.bfloat16)
    return high, (block - high.astype(jnp.float32)).astype(jnp.bfloat16)


def split_product(vectors, matrix_high, matrix_low, side):
    dims = (((1,), (side,)), ((), ()))
    dot = functools.partial(lax.dot_general, dimension_numbers=dims, preferred_element_type=jnp.float32)
    high, low = vectors
    if low is None:
        return dot(high, matrix_high) + dot(high, matrix_low)
    rows = high.shape[0]
    both = dot(jnp.concatenate([high, low], axis=0), matrix_high)
    return both[:rows] + both[rows:] + dot(high, matrix_low)


def parts_of(block, exact):
    if exact:
        return block.astype(jnp.bfloat16), None
    return halves(block)


def factor(matrix):
    size = matrix.shape[0]
    step = 8
    strips = size // step
    lane = lax.broadcasted_iota(jnp.int32, (step, size), 1)
    rows = [lax.broadcasted_iota(jnp.int32, (step, size), 0) + step * s for s in range(strips)]
    columns = [
        [jnp.broadcast_to(matrix[step * s : step * s + step, j : j + 1], (step, size)) for s in range(strips)]
        for j in range(size)
    ]
    inverse = [jnp.where(lane == rows[s], 1.0, 0.0) for s in range(strips)]
    lower = [jnp.zeros((step, size), jnp.float32) for _ in range(strips)]
    for k in range(size):
        home, at = divmod(k, step)
        pivot = jnp.broadcast_to(columns[k][home][at : at + 1, :], (step, size))
        root = lax.rsqrt(pivot)
        root = root * (1.5 - 0.5 * (pivot * root) * root)
        scaled = [None] * strips
        for s in range(home, strips):
            scaled[s] = columns[k][s] * root
            if s == home:
                scaled[s] = jnp.where(rows[s] >= k, scaled[s], 0.0)
            lower[s] = jnp.where(lane == k, scaled[s], lower[s])
        for j in range(k + 1, size):
            place, inside = divmod(j, step)
            weight = jnp.broadcast_to(scaled[place][inside : inside + 1, :], (step, size))
            for s in range(place, strips):
                columns[j][s] = columns[j][s] - scaled[s] * weight
        done = jnp.broadcast_to(inverse[home][at : at + 1, :], (step, size)) * root
        for s in range(home, strips):
            if s == home:
                inverse[s] = jnp.where(rows[s] == k, done, inverse[s] - jnp.where(rows[s] > k, scaled[s], 0.0) * done)
            else:
                inverse[s] = inverse[s] - scaled[s] * done
    return jnp.concatenate(lower, axis=0), jnp.concatenate(inverse, axis=0)


def pack(ref, place, matrix):
    side = matrix.shape[0]
    for q in range(side // PAD):
        start = SIDE * place + side * q
        ref[ref.shape[0] - PAD :, start : start + side] = matrix[PAD * q : PAD * q + PAD]


def unpack(ref, place, side):
    starts = [SIDE * place + side * q for q in range(side // PAD)]
    return jnp.concatenate([ref[ref.shape[0] - PAD :, s : s + side] for s in starts], axis=0)


def place_of(columns_ref, e):
    devices = lax.axis_size("col")
    position = lax.axis_index("col")
    core = position & 1
    ahead = core + lax.rem(columns_ref[0, e] - position + devices, devices)
    chip = ahead >> 1
    return core, (chip + 1) & 1, (chip - 1) >> 1, ahead & 1, chip == 0


def put_product(columns_ref, e, product, keep_ref, send_ref):
    core, speaker, part, block, here = place_of(columns_ref, e)
    slot = jnp.where(here, 1, part) * 2 + block

    @pl.when(speaker == core)
    def _():
        keep_ref[slot] = product

    @pl.when(speaker != core)
    def _():
        send_ref[slot] = product


def begin_kernel(
    columns_ref, probes_hbm, diagonal_hbm, forward_hbm,
    message_ref, core_ref, keep_ref, send_ref, high_ref, low_ref, diagonal_high_ref, diagonal_low_ref,
    probes_ref, diagonal_ref, forward_ref, sems,
):
    tiles = forward_ref.shape[0]
    copies = [pltpu.make_async_copy(probes_hbm, probes_ref, sems.at[0])]
    copies += [pltpu.make_async_copy(forward_hbm.at[e], forward_ref.at[e], sems.at[e + 1]) for e in range(tiles)]
    copies += [pltpu.make_async_copy(diagonal_hbm, diagonal_ref, sems.at[tiles + 1])]
    for copy in copies:
        copy.start()
    keep_ref[...] = jnp.zeros_like(keep_ref)
    send_ref[...] = jnp.zeros_like(send_ref)
    core_ref[...] = jnp.full(core_ref.shape, lax.axis_index("col") & 1, jnp.int32)
    copies[0].wait()
    signs = (2 * probes_ref[...] - 1).astype(jnp.float32) * SCALE
    rows, order = signs.shape
    message_ref[:rows] = signs
    gram = mm_t(signs, signs)
    exact = (signs.astype(jnp.bfloat16), None)
    for e in range(tiles):
        copies[e + 1].wait()
        high, low = halves(forward_ref[e])
        high_ref[e] = high
        low_ref[e] = low
        put_product(columns_ref, e, split_product(exact, high, low, 0), keep_ref, send_ref)
    copies[tiles + 1].wait()
    square = lax.broadcasted_iota(jnp.int32, (SIDE, SIDE), 0) == lax.broadcasted_iota(jnp.int32, (SIDE, SIDE), 1)
    trace = jnp.zeros((1, SIDE), jnp.float32)
    for start in range(0, order, SIDE):
        tile = diagonal_ref[start : start + SIDE, start : start + SIDE]
        trace += jnp.sum(jnp.where(square, tile, 0.0) * (1.0 / order), axis=0, keepdims=True)
    trace = jnp.sum(trace, axis=1, keepdims=True)
    message_ref[rows:] = jnp.broadcast_to(trace, (PAD, order))
    pack(message_ref, 0, gram)
    line = lax.broadcasted_iota(jnp.int32, (order, order), 0) == lax.broadcasted_iota(jnp.int32, (order, order), 1)
    high, low = halves(diagonal_ref[...] - jnp.where(line, trace, 0.0))
    diagonal_high_ref[...] = high
    diagonal_low_ref[...] = low


def outgoing_kernel(columns_ref, message_ref, high_ref, low_ref, keep_ref, send_ref):
    rows = keep_ref.shape[1]
    vectors = halves(message_ref[:rows])
    keep_ref[...] = jnp.zeros_like(keep_ref)
    send_ref[...] = jnp.zeros_like(send_ref)
    for e in range(high_ref.shape[0]):
        put_product(columns_ref, e, split_product(vectors, high_ref[e], low_ref[e], 0), keep_ref, send_ref)


def incoming_kernel(
    exact, columns_ref, message_ref, pair_ref, mine_ref, theirs_ref, high_ref, low_ref, diagonal_high_ref, diagonal_low_ref, image_ref
):
    rows = image_ref.shape[0]
    image = split_product(parts_of(message_ref[:rows], exact), diagonal_high_ref[...], diagonal_low_ref[...], 0)
    for e in range(high_ref.shape[0]):
        core, speaker, part, block, here = place_of(columns_ref, e)
        start = pl.multiple_of(jnp.where(here, 0, part) * 2 * rows + block * rows, rows)
        inside = pl.multiple_of(block * rows, rows)
        met = jnp.where(speaker == core, mine_ref[pl.ds(start, rows)], theirs_ref[pl.ds(start, rows)])
        met = jnp.where(here, pair_ref[pl.ds(inside, rows)], met)
        image += split_product(parts_of(met, exact), high_ref[e], low_ref[e], 1)
    image_ref[...] = image


def shift_of(devices, start_ref, sums_ref):
    mean = sums_ref[0:1, SIDE : SIDE + 1] * (1.0 / devices)
    return mean, start_ref[start_ref.shape[0] - PAD :][0:1, SIDE : SIDE + 1] - mean


def first_kernel(devices, start_ref, image_ref, total_ref, sums_ref, message_ref):
    rows, order = image_ref.shape
    signs = start_ref[:rows]
    image = image_ref[...] + total_ref[...] + shift_of(devices, start_ref, sums_ref)[1] * signs
    message_ref[:rows] = image
    both = mm_t(jnp.concatenate([signs, image], axis=0), image)
    message_ref[rows:] = jnp.zeros((PAD, order), jnp.float32)
    pack(message_ref, 0, both[:rows])
    pack(message_ref, 1, both[rows:])


def root_kernel(sums_ref, inverse_ref):
    inverse_ref[...] = factor(unpack(sums_ref, 0, inverse_ref.shape[0]))[1]


def second_kernel(
    devices, start_ref, message_ref, image_ref, total_ref, root_ref, first_sums_ref, sums_ref, basis_ref, result_ref, share_ref
):
    rows, order = image_ref.shape
    signs = start_ref[:rows]
    first = message_ref[:rows]
    mean, shift = shift_of(devices, start_ref, first_sums_ref)
    image = image_ref[...] + total_ref[...] + shift * first
    root = root_ref[...]
    alpha = mm_t(mm(root, unpack(sums_ref, 0, rows)), root)
    gram = mm_t(mm(root, unpack(sums_ref, 1, rows)), root) - mm_t(alpha, alpha)
    beta, inverse = factor(gram)
    scaled = mm(inverse, root)
    back = mm(mm(inverse, alpha), root)
    link = lax.dot_general(
        beta, root, (((0,), (0,)), ((), ())), precision=precise, preferred_element_type=jnp.float32
    )
    basis = mm(scaled, first) - mm(back, signs)
    result = mm(scaled, image) - mm(back, first) - mm(link, signs)
    basis_ref[...] = basis
    result_ref[...] = result
    both = mm_t(jnp.concatenate([basis, result], axis=0), result)
    line = lax.broadcasted_iota(jnp.int32, (rows, rows), 0)
    lane = lax.broadcasted_iota(jnp.int32, (rows, rows), 1)
    part = 1.0 / devices
    share_ref[:, :rows] = both[:rows]
    share_ref[:, rows : 2 * rows] = both[rows:]
    share_ref[:, 2 * rows : 3 * rows] = (alpha + jnp.where(line == lane, mean, 0.0)) * part
    share_ref[:, 3 * rows :] = jnp.where(lane > line, mean, beta) * part


def last_kernel(share_ref, basis_ref, result_ref, next_ref, blocks_ref):
    rows = share_ref.shape[0]
    line = lax.broadcasted_iota(jnp.int32, (rows, rows), 0)
    lane = lax.broadcasted_iota(jnp.int32, (rows, rows), 1)
    alpha = share_ref[:, :rows]
    mean = share_ref[0:1, 4 * rows - 1 : 4 * rows]
    gram = share_ref[:, rows : 2 * rows] - mm_t(alpha, alpha)
    beta, inverse = factor(gram)
    next_ref[...] = mm(inverse, result_ref[...] - mm(alpha, basis_ref[...]))
    blocks_ref[0] = share_ref[:, 2 * rows : 3 * rows]
    blocks_ref[1] = jnp.where(lane > line, 0.0, share_ref[:, 3 * rows :])
    blocks_ref[2] = alpha + jnp.where(line == lane, mean, 0.0)
    blocks_ref[3] = beta


def call(kernel, out_shape, args, smem=0, hbm=0, scratch=(), room=8):
    args = [pltpu.with_memory_space_constraint(a, pltpu.HBM) if j < smem + hbm else a for j, a in enumerate(args)]
    outs = in_vmem if not isinstance(out_shape, tuple) else (in_vmem,) * len(out_shape)
    return pl.pallas_call(
        kernel,
        out_shape=out_shape,
        in_specs=[in_smem] * smem + [in_hbm] * hbm + [in_vmem] * (len(args) - smem - hbm),
        out_specs=outs,
        scratch_shapes=list(scratch),
        compiler_params=pltpu.CompilerParams(vmem_limit_bytes=room * 1024 * 1024),
        cost_estimate=pl.CostEstimate(flops=1, bytes_accessed=1, transcendentals=0),
    )(*args)


def body(probes, diagonal, forward_tiles, tile_columns):
    forward = forward_tiles[0]
    rows, order = probes.shape
    devices = lax.axis_size("col")

    def swapped(block, bits=1):
        return lax.ppermute(block, "col", [(i ^ bits, i) for i in range(devices)])

    def from_chips(block, *chips):
        hops = [chips[i & 1] for i in range(devices)]
        route = [((i + 2 * hops[i]) % devices, i) for i in range(devices) if hops[i] is not None]
        return lax.ppermute(block, "col", route)

    def whole(sums):
        bits = 2
        while bits < devices:
            sums = sums + swapped(sums, bits)
            bits *= 2
        return sums

    def apply(message, products, exact):
        partner = swapped(message)
        pair = jnp.concatenate(
            [
                jnp.where(lower, message[:rows], partner[:rows]),
                jnp.where(lower, partner[:rows], message[:rows]),
                message[rows:] + partner[rows:],
            ]
        )
        payload = pair[2 * rows :]
        near, far = from_chips(pair, 1, 2), from_chips(pair, 3, None)
        last = from_chips(jnp.concatenate([pair[:rows], payload]), None, 4)
        if products is None:
            message, pair = lax.optimization_barrier((message, pair))
            products = call(
                outgoing_kernel,
                (struct(4, rows, order), struct(4, rows, order)),
                (tile_columns, message, high, low),
                smem=1,
            )
        keep, send = products
        ahead = keep + swapped(send)
        near_ahead = jnp.concatenate([ahead[0], ahead[1], payload])
        far_ahead = jnp.concatenate([ahead[2], ahead[3], payload])
        near_back, far_back = from_chips(near_ahead, -1, -2), from_chips(far_ahead, -3, None)
        last_back = from_chips(ahead[2], None, -4)
        near, far, last, near_back, far_back, last_back = lax.optimization_barrier(
            (near, far, last, near_back, far_back, last_back)
        )
        mine = jnp.concatenate([near[: 2 * rows], far[:rows] + last[:rows], far[rows : 2 * rows]])
        theirs = swapped(mine)
        image = call(
            functools.partial(incoming_kernel, exact),
            struct(rows, order),
            (tile_columns, message, pair, mine, theirs, high, low, diagonal_high, diagonal_low),
            smem=1,
        )
        if devices == 16:
            sums = jnp.where(lower_pad, payload, 0.0) + near[2 * rows :] + far[2 * rows :] + last[rows:]
            sums = sums + near_back[2 * rows :] + far_back[2 * rows :]
        else:
            sums = jnp.where(lower_pad, whole(payload), 0.0)
        first = near_back[:rows] + far_back[:rows] + last_back
        second = near_back[rows : 2 * rows] + jnp.where(lower, far_back[rows : 2 * rows], far_ahead[rows : 2 * rows])
        other = swapped(jnp.concatenate([jnp.where(lower, second, first), sums]))
        return image, jnp.where(lower, first, second) + other[:rows], sums + other[rows:]

    tiles = forward.shape[0]
    split = pltpu.VMEM(forward.shape, jnp.bfloat16)
    split_diagonal = pltpu.VMEM(diagonal.shape, jnp.bfloat16)
    start, core, keep, send, high, low, diagonal_high, diagonal_low = call(
        begin_kernel,
        (
            struct(rows + PAD, order), pltpu.VMEM((rows, order), jnp.int32),
            struct(4, rows, order), struct(4, rows, order),
            split, split, split_diagonal, split_diagonal,
        ),
        (tile_columns, probes, diagonal, forward),
        smem=1,
        hbm=3,
        room=12,
        scratch=(
            pltpu.VMEM(probes.shape, jnp.int32),
            pltpu.VMEM(diagonal.shape, jnp.float32),
            pltpu.VMEM(forward.shape, jnp.float32),
            pltpu.SemaphoreType.DMA((tiles + 2,)),
        ),
    )
    lower = core == 0
    lower_pad = lower[:PAD]
    image, total, start_sums = apply(start, (keep, send), True)
    message = call(
        functools.partial(first_kernel, devices), struct(rows + PAD, order), (start, image, total, start_sums)
    )
    image, total, sums = apply(message, None, False)
    root = call(root_kernel, struct(rows, rows), (start_sums,))
    basis, result, share = call(
        functools.partial(second_kernel, devices),
        (struct(rows, order), struct(rows, order), struct(rows, SIDE)),
        (start, message, image, total, root, start_sums, sums),
    )
    bits = 1
    while bits < devices:
        if 4 * bits <= devices:
            one, two, three = (swapped(share, bits * j) for j in (1, 2, 3))
            share = (share + one) + (two + three)
            bits *= 4
        else:
            share = share + swapped(share, bits)
            bits *= 2
    outs = (jax.ShapeDtypeStruct((rows, order), jnp.float32), jax.ShapeDtypeStruct((4, rows, rows), jnp.float32))
    return call(last_kernel, outs, (share, basis, result))


def solution(mesh):
    placed = (
        P(None, ("groups", "col")),
        P(("groups", "col"), None),
        P(("groups", "col"), None, None, None),
        P(("groups", "col"), None),
    )
    return jax.shard_map(
        body,
        mesh=mesh,
        in_specs=placed,
        out_specs=(P(None, ("groups", "col")), P("groups", None, None)),
        check_vma=False,
    )
```

```python
import functools

import jax
import jax.numpy as jnp
from jax import lax
from jax.experimental import pallas as pl
from jax.experimental.pallas import tpu as pltpu
from jax.sharding import PartitionSpec as P

SCALE = 0.0078125
SIDE = 128
PAD = 8
SLOTS = 6

precise = lax.Precision.HIGHEST
in_vmem = pl.BlockSpec(memory_space=pltpu.VMEM)
in_hbm = pl.BlockSpec(memory_space=pltpu.HBM)
in_smem = pl.BlockSpec(memory_space=pltpu.SMEM)


def struct(*shape):
    return pltpu.VMEM(shape, jnp.float32)


def mm(left, right):
    return lax.dot_general(
        left, right, (((1,), (0,)), ((), ())), precision=precise, preferred_element_type=jnp.float32
    )


def mm_t(left, right):
    return lax.dot_general(
        left, right, (((1,), (1,)), ((), ())), precision=precise, preferred_element_type=jnp.float32
    )


def halves(block):
    high = block.astype(jnp.bfloat16)
    return high, (block - high.astype(jnp.float32)).astype(jnp.bfloat16)


def split_product(vectors, matrix_high, matrix_low, side):
    dims = (((1,), (side,)), ((), ()))
    dot = functools.partial(lax.dot_general, dimension_numbers=dims, preferred_element_type=jnp.float32)
    high, low = vectors
    if low is None:
        return dot(high, matrix_high) + dot(high, matrix_low)
    rows = high.shape[0]
    both = dot(jnp.concatenate([high, low], axis=0), matrix_high)
    return both[:rows] + both[rows:] + dot(high, matrix_low)


def parts_of(block, exact):
    if exact:
        return block.astype(jnp.bfloat16), None
    return halves(block)


def factor(matrix):
    size = matrix.shape[0]
    step = 8
    strips = size // step
    lane = lax.broadcasted_iota(jnp.int32, (step, size), 1)
    rows = [lax.broadcasted_iota(jnp.int32, (step, size), 0) + step * s for s in range(strips)]
    columns = [
        [jnp.broadcast_to(matrix[step * s : step * s + step, j : j + 1], (step, size)) for s in range(strips)]
        for j in range(size)
    ]
    inverse = [jnp.where(lane == rows[s], 1.0, 0.0) for s in range(strips)]
    lower = [jnp.zeros((step, size), jnp.float32) for _ in range(strips)]
    for k in range(size):
        home, at = divmod(k, step)
        pivot = jnp.broadcast_to(columns[k][home][at : at + 1, :], (step, size))
        root = lax.rsqrt(pivot)
        root = root * (1.5 - 0.5 * (pivot * root) * root)
        scaled = [None] * strips
        for s in range(home, strips):
            scaled[s] = columns[k][s] * root
            if s == home:
                scaled[s] = jnp.where(rows[s] >= k, scaled[s], 0.0)
            lower[s] = jnp.where(lane == k, scaled[s], lower[s])
        for j in range(k + 1, size):
            place, inside = divmod(j, step)
            weight = jnp.broadcast_to(scaled[place][inside : inside + 1, :], (step, size))
            for s in range(place, strips):
                columns[j][s] = columns[j][s] - scaled[s] * weight
        done = jnp.broadcast_to(inverse[home][at : at + 1, :], (step, size)) * root
        for s in range(home, strips):
            if s == home:
                inverse[s] = jnp.where(rows[s] == k, done, inverse[s] - jnp.where(rows[s] > k, scaled[s], 0.0) * done)
            else:
                inverse[s] = inverse[s] - scaled[s] * done
    return jnp.concatenate(lower, axis=0), jnp.concatenate(inverse, axis=0)


def pack(ref, base, place, matrix):
    side = matrix.shape[0]
    for q in range(side // PAD):
        start = SIDE * place + side * q
        ref[base : base + PAD, start : start + side] = matrix[PAD * q : PAD * q + PAD]


def unpack(ref, place, side):
    starts = [SIDE * place + side * q for q in range(side // PAD)]
    return jnp.concatenate([ref[:, s : s + side] for s in starts], axis=0)


def place_of(columns_ref, e):
    devices = lax.axis_size("col")
    position = lax.axis_index("col")
    core = position & 1
    ahead = core + lax.rem(columns_ref[0, e] - position + devices, devices)
    return core, ahead >> 1, ahead & 1


def place_products(columns_ref, products_ref, bundle_ref, keep_ref):
    rows = products_ref.shape[1]
    start = rows + PAD
    keep_ref[...] = jnp.zeros_like(keep_ref)
    bundle_ref[start:] = jnp.zeros((bundle_ref.shape[0] - start, bundle_ref.shape[1]), jnp.float32)
    for e in range(products_ref.shape[0]):
        core, chip, block = place_of(columns_ref, e)
        speaker = jnp.where(chip == 1, 0, 1)
        slot = jnp.where(chip == 0, SLOTS - 1, jnp.where(chip < 3, 0, 2 * chip - 4) + block)

        @pl.when(speaker == core)
        def _():
            keep_ref[slot] = products_ref[e]

        @pl.when(speaker != core)
        def _():
            bundle_ref[pl.ds(pl.multiple_of(start + slot * rows, PAD), rows)] = products_ref[e]


def begin_kernel(
    columns_ref, probes_hbm, diagonal_hbm, forward_hbm,
    bundle_ref, core_ref, keep_ref, high_ref, low_ref,
    probes_ref, diagonal_ref, forward_ref, products_ref, sems,
):
    tiles = forward_ref.shape[0]
    squares = diagonal_ref.shape[0]
    copies = [pltpu.make_async_copy(probes_hbm, probes_ref, sems.at[0])]
    for q in range(squares):
        ends = pl.ds(SIDE * q, SIDE)
        copies += [pltpu.make_async_copy(diagonal_hbm.at[ends, ends], diagonal_ref.at[q], sems.at[1 + q])]
    for e in range(tiles):
        copies += [pltpu.make_async_copy(forward_hbm.at[e], forward_ref.at[e], sems.at[1 + squares + e])]
    for copy in copies:
        copy.start()
    core_ref[...] = jnp.full(core_ref.shape, lax.axis_index("col") & 1, jnp.int32)
    copies[0].wait()
    signs = (2 * probes_ref[...] - 1).astype(jnp.float32) * SCALE
    rows, order = signs.shape
    bundle_ref[:rows] = signs
    square = lax.broadcasted_iota(jnp.int32, (SIDE, SIDE), 0) == lax.broadcasted_iota(jnp.int32, (SIDE, SIDE), 1)
    trace = jnp.zeros((SIDE, SIDE), jnp.float32)
    for q in range(squares):
        copies[1 + q].wait()
        trace += jnp.where(square, diagonal_ref[q], 0.0) * (1.0 / order)
    trace = jnp.sum(jnp.sum(trace, axis=0, keepdims=True), axis=1, keepdims=True)
    bundle_ref[rows : rows + PAD] = jnp.broadcast_to(trace, (PAD, order))
    pack(bundle_ref, rows, 0, mm_t(signs, signs))
    exact = (signs.astype(jnp.bfloat16), None)
    for e in range(tiles):
        copies[1 + squares + e].wait()
        high, low = halves(forward_ref[e])
        high_ref[e] = high
        low_ref[e] = low
        products_ref[e] = split_product(exact, high, low, 0)
    place_products(columns_ref, products_ref, bundle_ref, keep_ref)


def first_near_kernel(
    bundle_ref, diagonal_ref, tile_high_ref, tile_low_ref, image_ref, high_ref, low_ref, turned_high_ref, turned_low_ref
):
    rows, order = image_ref.shape
    trace = bundle_ref[rows : rows + 1, SIDE : SIDE + 1]
    line = lax.broadcasted_iota(jnp.int32, (order, order), 0) == lax.broadcasted_iota(jnp.int32, (order, order), 1)
    high, low = halves(diagonal_ref[...] - jnp.where(line, trace, 0.0))
    high_ref[...] = high
    low_ref[...] = low
    image_ref[...] = split_product(parts_of(bundle_ref[:rows], True), high, low, 0)
    for e in range(tile_high_ref.shape[0]):
        turned_high_ref[e] = tile_high_ref[e].T
        turned_low_ref[e] = tile_low_ref[e].T


def second_near_kernel(bundle_ref, high_ref, low_ref, image_ref):
    rows = image_ref.shape[0]
    image_ref[...] = split_product(parts_of(bundle_ref[:rows], False), high_ref[...], low_ref[...], 0)


def incoming_kernel(exact, columns_ref, pair_ref, mine_ref, theirs_ref, high_ref, low_ref, image_ref, ready_ref):
    rows = image_ref.shape[0]
    tiles = high_ref.shape[0]
    for e in range(tiles):
        core, chip, block = place_of(columns_ref, e)
        speaker = jnp.where(chip == 2, 1, 0)
        part = jnp.where(chip < 3, 0, 2 * chip - 4)
        start = pl.multiple_of((part + block) * rows, rows)
        inside = pl.multiple_of(block * rows, rows)
        met = jnp.where(speaker == core, mine_ref[pl.ds(start, rows)], theirs_ref[pl.ds(start, rows)])
        met = jnp.where(chip == 0, pair_ref[pl.ds(inside, rows)], met)
        high, low = parts_of(met, exact)
        ready_ref[e, :rows] = high
        if not exact:
            ready_ref[e, rows:] = low
    image = jnp.zeros(image_ref.shape, jnp.float32)
    for e in range(tiles):
        vectors = ready_ref[e, :rows], None if exact else ready_ref[e, rows:]
        image += split_product(vectors, high_ref[e], low_ref[e], 0)
    image_ref[...] = image


def shift_of(devices, start_ref, sums_ref, rows):
    mean = sums_ref[0:1, SIDE : SIDE + 1] * (1.0 / devices)
    return mean, start_ref[rows : rows + 1, SIDE : SIDE + 1] - mean


def first_kernel(
    devices, columns_ref, start_ref, near_ref, image_ref, total_ref, sums_ref, high_ref, low_ref,
    bundle_ref, keep_ref, products_ref,
):
    rows, order = image_ref.shape
    signs = start_ref[:rows]
    image = near_ref[...] + image_ref[...] + total_ref[...]
    image += shift_of(devices, start_ref, sums_ref, rows)[1] * signs
    bundle_ref[:rows] = image
    vectors = halves(image)
    for e in range(high_ref.shape[0]):
        products_ref[e] = split_product(vectors, high_ref[e], low_ref[e], 0)
    both = mm_t(jnp.concatenate([signs, image], axis=0), image)
    bundle_ref[rows : rows + PAD] = jnp.zeros((PAD, order), jnp.float32)
    pack(bundle_ref, rows, 0, both[:rows])
    pack(bundle_ref, rows, 1, both[rows:])
    place_products(columns_ref, products_ref, bundle_ref, keep_ref)


def root_kernel(sums_ref, start_ref, message_ref, root_ref, lines_ref):
    rows = root_ref.shape[0]
    root = factor(unpack(sums_ref, 0, rows))[1]
    root_ref[...] = root
    lines_ref[...] = mm(root, jnp.concatenate([start_ref[:rows], message_ref[:rows]], axis=1))


def second_kernel(
    devices, start_ref, message_ref, near_ref, image_ref, total_ref, root_ref, lines_ref, first_sums_ref, sums_ref,
    basis_ref, result_ref, share_ref,
):
    rows, order = image_ref.shape
    mean, shift = shift_of(devices, start_ref, first_sums_ref, rows)
    root = root_ref[...]
    alpha = mm_t(mm(root, unpack(sums_ref, 0, rows)), root)
    gram = mm_t(mm(root, unpack(sums_ref, 1, rows)), root) - mm_t(alpha, alpha)
    image = mm(root, near_ref[...] + image_ref[...] + total_ref[...] + shift * message_ref[:rows])
    first_basis, first = lines_ref[:, :order], lines_ref[:, order:]
    bent = mm(alpha, lines_ref[...])
    beta, inverse = factor(gram)
    both = mm(inverse, jnp.concatenate([first - bent[:, :order], image - bent[:, order:]], axis=1))
    link = lax.dot_general(
        beta, first_basis, (((0,), (0,)), ((), ())), precision=precise, preferred_element_type=jnp.float32
    )
    basis = both[:, :order]
    result = both[:, order:] - link
    basis_ref[...] = basis
    result_ref[...] = result
    both = mm_t(jnp.concatenate([basis, result], axis=0), result)
    line = lax.broadcasted_iota(jnp.int32, (rows, rows), 0)
    lane = lax.broadcasted_iota(jnp.int32, (rows, rows), 1)
    part = 1.0 / devices
    share_ref[:, :rows] = both[:rows]
    share_ref[:, rows : 2 * rows] = both[rows:]
    share_ref[:, 2 * rows : 3 * rows] = (alpha + jnp.where(line == lane, mean, 0.0)) * part
    share_ref[:, 3 * rows :] = jnp.where(lane > line, mean, beta) * part


def last_kernel(share_ref, basis_ref, result_ref, next_ref, blocks_ref):
    rows = share_ref.shape[0]
    line = lax.broadcasted_iota(jnp.int32, (rows, rows), 0)
    lane = lax.broadcasted_iota(jnp.int32, (rows, rows), 1)
    alpha = share_ref[:, :rows]
    mean = share_ref[0:1, 4 * rows - 1 : 4 * rows]
    gram = share_ref[:, rows : 2 * rows] - mm_t(alpha, alpha)
    beta, inverse = factor(gram)
    next_ref[...] = mm(inverse, result_ref[...] - mm(alpha, basis_ref[...]))
    blocks_ref[0] = share_ref[:, 2 * rows : 3 * rows]
    blocks_ref[1] = jnp.where(lane > line, 0.0, share_ref[:, 3 * rows :])
    blocks_ref[2] = alpha + jnp.where(line == lane, mean, 0.0)
    blocks_ref[3] = beta


def call(kernel, out_shape, args, smem=0, hbm=0, scratch=(), room=8):
    args = [pltpu.with_memory_space_constraint(a, pltpu.HBM) if j < smem + hbm else a for j, a in enumerate(args)]
    outs = in_vmem if not isinstance(out_shape, tuple) else (in_vmem,) * len(out_shape)
    return pl.pallas_call(
        kernel,
        out_shape=out_shape,
        in_specs=[in_smem] * smem + [in_hbm] * hbm + [in_vmem] * (len(args) - smem - hbm),
        out_specs=outs,
        scratch_shapes=list(scratch),
        compiler_params=pltpu.CompilerParams(vmem_limit_bytes=room * 1024 * 1024),
        cost_estimate=pl.CostEstimate(flops=1, bytes_accessed=1, transcendentals=0),
    )(*args)


def body(probes, diagonal, forward_tiles, tile_columns):
    forward = forward_tiles[0]
    rows, order = probes.shape
    devices = lax.axis_size("col")

    def swapped(block, bits=1):
        return lax.ppermute(block, "col", [(i ^ bits, i) for i in range(devices)])

    def from_chips(block, *chips):
        hops = [chips[i & 1] for i in range(devices)]
        route = [((i + 2 * hops[i]) % devices, i) for i in range(devices) if hops[i] is not None]
        return lax.ppermute(block, "col", route)

    def whole(sums):
        bits = 2
        while bits < devices:
            sums = sums + swapped(sums, bits)
            bits *= 2
        return sums

    def apply(bundle, keep, near_call, exact):
        partner = swapped(bundle)
        own, its = bundle[:rows], partner[:rows]
        payload = bundle[rows:top] + partner[rows:top]
        pair = jnp.concatenate([jnp.where(lower, own, its), jnp.where(lower, its, own), payload])
        ahead = keep + partner[top:].reshape(keep.shape)
        near_ahead = jnp.concatenate([ahead[0], ahead[1], payload])
        third_ahead = jnp.concatenate([ahead[2], ahead[3]])
        third_ahead = jnp.concatenate([jnp.where(both_lower, pair[: 2 * rows], third_ahead), payload])
        fourth_ahead = jnp.concatenate([jnp.where(lower, pair[:rows], ahead[4]), payload])
        near = from_chips(pair, 1, 2)
        near_back = from_chips(near_ahead, -1, -2)
        third = from_chips(third_ahead, 3, -3)
        fourth = from_chips(fourth_ahead, 4, -4)
        bundle, _, _ = lax.optimization_barrier((bundle, near_ahead, third_ahead))
        inner, turned = near_call(bundle)
        near, near_back, third, fourth, inner, turned = lax.optimization_barrier(
            (near, near_back, third, fourth, inner, turned)
        )
        mine = jnp.concatenate([near[: 2 * rows], third[: 2 * rows], fourth[:rows]])
        if devices == 16:
            sums = near[2 * rows :] + near_back[2 * rows :] + third[2 * rows :]
            sums = sums + jnp.where(lower_pad, payload + fourth[rows:], 0.0)
        else:
            sums = jnp.where(lower_pad, whole(payload), 0.0)
        first = near_back[:rows] + jnp.where(lower, 0.0, third[:rows] + fourth[:rows])
        second = near_back[rows : 2 * rows] + jnp.where(lower, 0.0, third[rows : 2 * rows] + ahead[SLOTS - 1])
        other = jnp.concatenate([jnp.where(lower, second, first), sums])
        mine, other = lax.optimization_barrier((mine, other))
        theirs, other = swapped(mine), swapped(other)
        image = call(
            functools.partial(incoming_kernel, exact),
            struct(rows, order),
            (tile_columns, pair, mine, theirs, *turned[-2:]),
            smem=1,
            scratch=(pltpu.VMEM((tiles, 2 * rows, order), jnp.bfloat16),),
        )
        return inner, image, jnp.where(lower, first, second) + other[:rows], sums + other[rows:], turned

    tiles = forward.shape[0]
    top = rows + PAD
    bundles = (struct(top + SLOTS * rows, order), struct(SLOTS, rows, order))
    products = pltpu.VMEM((tiles, rows, order), jnp.float32)
    split = pltpu.VMEM(forward.shape, jnp.bfloat16)
    split_diagonal = pltpu.VMEM(diagonal.shape, jnp.bfloat16)
    start, core, keep, high, low = call(
        begin_kernel,
        (bundles[0], pltpu.VMEM((rows, order), jnp.int32), bundles[1], split, split),
        (tile_columns, probes, diagonal, forward),
        smem=1,
        hbm=3,
        room=12,
        scratch=(
            pltpu.VMEM(probes.shape, jnp.int32),
            pltpu.VMEM((order // SIDE, SIDE, SIDE), jnp.float32),
            pltpu.VMEM(forward.shape, jnp.float32),
            products,
            pltpu.SemaphoreType.DMA((tiles + 1 + order // SIDE,)),
        ),
    )
    lower = core == 0
    lower_pad = lower[:PAD]
    both_lower = jnp.concatenate([lower, lower])

    def first_near(bundle):
        made = call(
            first_near_kernel,
            (struct(rows, order), split_diagonal, split_diagonal, split, split),
            (bundle, diagonal, high, low),
        )
        return made[0], made[1:]

    inner, image, total, start_sums, turned = apply(start, keep, first_near, True)
    diagonal_high, diagonal_low, *turned = turned
    message, keep = call(
        functools.partial(first_kernel, devices),
        bundles,
        (tile_columns, start, inner, image, total, start_sums, high, low),
        smem=1,
        scratch=(products,),
    )
    def second_near(bundle):
        inner = call(second_near_kernel, struct(rows, order), (bundle, diagonal_high, diagonal_low))
        ahead = call(root_kernel, (struct(rows, rows), struct(rows, 2 * order)), (start_sums, start, bundle))
        return inner, (*ahead, *turned)

    inner, image, total, sums, (root, lines, *_) = apply(message, keep, second_near, False)
    basis, result, share = call(
        functools.partial(second_kernel, devices),
        (struct(rows, order), struct(rows, order), struct(rows, SIDE)),
        (start, message, inner, image, total, root, lines, start_sums, sums),
    )
    bits = 1
    while bits < devices:
        if 4 * bits <= devices:
            one, two, three = (swapped(share, bits * j) for j in (1, 2, 3))
            share = (share + one) + (two + three)
            bits *= 4
        else:
            share = share + swapped(share, bits)
            bits *= 2
    outs = (jax.ShapeDtypeStruct((rows, order), jnp.float32), jax.ShapeDtypeStruct((4, rows, rows), jnp.float32))
    return call(last_kernel, outs, (share, basis, result))


def solution(mesh):
    placed = (
        P(None, ("groups", "col")),
        P(("groups", "col"), None),
        P(("groups", "col"), None, None, None),
        P(("groups", "col"), None),
    )
    return jax.shard_map(
        body,
        mesh=mesh,
        in_specs=placed,
        out_specs=(P(None, ("groups", "col")), P("groups", None, None)),
        check_vma=False,
    )
```

```python
import functools

import jax
import jax.numpy as jnp
from jax import lax
from jax.experimental import pallas as pl
from jax.experimental.pallas import tpu as pltpu
from jax.sharding import PartitionSpec as P

SCALE = 0.0078125
SIDE = 128
PAD = 8
SLOTS = 6
NOTES = 2

precise = lax.Precision.HIGHEST
in_vmem = pl.BlockSpec(memory_space=pltpu.VMEM)
in_hbm = pl.BlockSpec(memory_space=pltpu.HBM)
in_smem = pl.BlockSpec(memory_space=pltpu.SMEM)


def struct(*shape):
    return pltpu.VMEM(shape, jnp.float32)


def mm(left, right):
    return lax.dot_general(
        left, right, (((1,), (0,)), ((), ())), precision=precise, preferred_element_type=jnp.float32
    )


def mm_t(left, right):
    return lax.dot_general(
        left, right, (((1,), (1,)), ((), ())), precision=precise, preferred_element_type=jnp.float32
    )


def halves(block):
    high = block.astype(jnp.bfloat16)
    return high, (block - high.astype(jnp.float32)).astype(jnp.bfloat16)


def split_product(vectors, matrix_high, matrix_low, side):
    dims = (((1,), (side,)), ((), ()))
    dot = functools.partial(lax.dot_general, dimension_numbers=dims, preferred_element_type=jnp.float32)
    high, low = vectors
    if low is None:
        return dot(high, matrix_high) + dot(high, matrix_low)
    rows = high.shape[0]
    both = dot(jnp.concatenate([high, low], axis=0), matrix_high)
    return both[:rows] + both[rows:] + dot(high, matrix_low)


def parts_of(block, exact):
    if exact:
        return block.astype(jnp.bfloat16), None
    return halves(block)


def factor(matrix):
    size = matrix.shape[0]
    step = 8
    strips = size // step
    lane = lax.broadcasted_iota(jnp.int32, (step, size), 1)
    rows = [lax.broadcasted_iota(jnp.int32, (step, size), 0) + step * s for s in range(strips)]
    columns = [
        [jnp.broadcast_to(matrix[step * s : step * s + step, j : j + 1], (step, size)) for s in range(strips)]
        for j in range(size)
    ]
    inverse = [jnp.where(lane == rows[s], 1.0, 0.0) for s in range(strips)]
    lower = [jnp.zeros((step, size), jnp.float32) for _ in range(strips)]
    for k in range(size):
        home, at = divmod(k, step)
        pivot = jnp.broadcast_to(columns[k][home][at : at + 1, :], (step, size))
        root = lax.rsqrt(pivot)
        root = root * (1.5 - 0.5 * (pivot * root) * root)
        scaled = [None] * strips
        for s in range(home, strips):
            scaled[s] = columns[k][s] * root
            if s == home:
                scaled[s] = jnp.where(rows[s] >= k, scaled[s], 0.0)
            lower[s] = jnp.where(lane == k, scaled[s], lower[s])
        for j in range(k + 1, size):
            place, inside = divmod(j, step)
            weight = jnp.broadcast_to(scaled[place][inside : inside + 1, :], (step, size))
            for s in range(place, strips):
                columns[j][s] = columns[j][s] - scaled[s] * weight
        done = jnp.broadcast_to(inverse[home][at : at + 1, :], (step, size)) * root
        for s in range(home, strips):
            if s == home:
                inverse[s] = jnp.where(rows[s] == k, done, inverse[s] - jnp.where(rows[s] > k, scaled[s], 0.0) * done)
            else:
                inverse[s] = inverse[s] - scaled[s] * done
    return jnp.concatenate(lower, axis=0), jnp.concatenate(inverse, axis=0)


def pack(matrix):
    return jnp.concatenate([matrix[q : q + PAD] for q in range(0, matrix.shape[0], PAD)], axis=1)


def unpack(tile, side):
    return jnp.concatenate([tile[:, q : q + side] for q in range(0, SIDE, side)], axis=0)


def join(tiles, wide):
    rows = [jnp.concatenate([tiles[q + j] for j in range(wide)], axis=1) for q in range(0, tiles.shape[0], wide)]
    return jnp.concatenate(rows, axis=0)


def put(ref, base, block):
    wide = block.shape[1] // SIDE
    for i in range(block.shape[0] // PAD):
        for j in range(wide):
            ref[base + wide * i + j] = block[PAD * i : PAD * i + PAD, SIDE * j : SIDE * j + SIDE]


def block_of(ref, shape):
    rows, order = shape
    return join(ref[: rows * order // (PAD * SIDE)], order // SIDE)


def place_of(columns_ref, e):
    devices = lax.axis_size("col")
    position = lax.axis_index("col")
    core = position & 1
    ahead = core + lax.rem(columns_ref[0, e] - position + devices, devices)
    return core, ahead >> 1, ahead & 1


def place_products(columns_ref, products_ref, bundle_ref, keep_ref):
    size = keep_ref.shape[0] // SLOTS
    start = size + NOTES
    keep_ref[...] = jnp.zeros_like(keep_ref)
    bundle_ref[start:] = jnp.zeros_like(keep_ref)
    for e in range(products_ref.shape[0]):
        core, chip, block = place_of(columns_ref, e)
        speaker = jnp.where(chip == 1, 0, 1)
        slot = jnp.where(chip == 0, SLOTS - 1, jnp.where(chip < 3, 0, 2 * chip - 4) + block)

        @pl.when(speaker == core)
        def _():
            put(keep_ref, slot * size, products_ref[e])

        @pl.when(speaker != core)
        def _():
            put(bundle_ref, start + slot * size, products_ref[e])


def begin_kernel(
    columns_ref, probes_hbm, diagonal_hbm, forward_hbm,
    bundle_ref, core_ref, keep_ref, high_ref, low_ref,
    probes_ref, diagonal_ref, forward_ref, products_ref, sems,
):
    tiles = forward_ref.shape[0]
    squares = diagonal_ref.shape[0]
    copies = [pltpu.make_async_copy(probes_hbm, probes_ref, sems.at[0])]
    for q in range(squares):
        ends = pl.ds(SIDE * q, SIDE)
        copies += [pltpu.make_async_copy(diagonal_hbm.at[ends, ends], diagonal_ref.at[q], sems.at[1 + q])]
    for e in range(tiles):
        copies += [pltpu.make_async_copy(forward_hbm.at[e], forward_ref.at[e], sems.at[1 + squares + e])]
    for copy in copies:
        copy.start()
    core_ref[...] = jnp.full(core_ref.shape, lax.axis_index("col") & 1, jnp.int32)
    copies[0].wait()
    signs = (2 * probes_ref[...] - 1).astype(jnp.float32) * SCALE
    rows, order = signs.shape
    size = rows * order // (PAD * SIDE)
    put(bundle_ref, 0, signs)
    square = lax.broadcasted_iota(jnp.int32, (SIDE, SIDE), 0) == lax.broadcasted_iota(jnp.int32, (SIDE, SIDE), 1)
    trace = jnp.zeros((SIDE, SIDE), jnp.float32)
    for q in range(squares):
        copies[1 + q].wait()
        trace += jnp.where(square, diagonal_ref[q], 0.0) * (1.0 / order)
    trace = jnp.sum(jnp.sum(trace, axis=0, keepdims=True), axis=1, keepdims=True)
    bundle_ref[size] = pack(mm_t(signs, signs))
    bundle_ref[size + 1] = jnp.broadcast_to(trace, (PAD, SIDE))
    exact = (signs.astype(jnp.bfloat16), None)
    for e in range(tiles):
        copies[1 + squares + e].wait()
        high, low = halves(forward_ref[e])
        high_ref[e] = high
        low_ref[e] = low
        products_ref[e] = split_product(exact, high, low, 0)
    place_products(columns_ref, products_ref, bundle_ref, keep_ref)


def first_near_kernel(
    bundle_ref, diagonal_ref, tile_high_ref, tile_low_ref, image_ref, high_ref, low_ref, turned_high_ref, turned_low_ref
):
    rows, order = image_ref.shape
    trace = bundle_ref[rows * order // (PAD * SIDE) + 1, 0:1, 0:1]
    line = lax.broadcasted_iota(jnp.int32, (order, order), 0) == lax.broadcasted_iota(jnp.int32, (order, order), 1)
    high, low = halves(diagonal_ref[...] - jnp.where(line, trace, 0.0))
    high_ref[...] = high
    low_ref[...] = low
    image_ref[...] = split_product(parts_of(block_of(bundle_ref, image_ref.shape), True), high, low, 0)
    for e in range(tile_high_ref.shape[0]):
        turned_high_ref[e] = tile_high_ref[e].T
        turned_low_ref[e] = tile_low_ref[e].T


def second_near_kernel(bundle_ref, high_ref, low_ref, image_ref):
    image_ref[...] = split_product(parts_of(block_of(bundle_ref, image_ref.shape), False), high_ref[...], low_ref[...], 0)


def incoming_kernel(exact, columns_ref, pair_ref, mine_ref, theirs_ref, high_ref, low_ref, image_ref, ready_ref):
    rows, order = image_ref.shape
    size = rows * order // (PAD * SIDE)
    tiles = high_ref.shape[0]
    for e in range(tiles):
        core, chip, block = place_of(columns_ref, e)
        speaker = jnp.where(chip == 2, 1, 0)
        part = jnp.where(chip < 3, 0, 2 * chip - 4)
        met = jnp.where(
            speaker == core, mine_ref[pl.ds((part + block) * size, size)], theirs_ref[pl.ds((part + block) * size, size)]
        )
        met = join(jnp.where(chip == 0, pair_ref[pl.ds(block * size, size)], met), order // SIDE)
        high, low = parts_of(met, exact)
        ready_ref[e, :rows] = high
        if not exact:
            ready_ref[e, rows:] = low
    image = jnp.zeros(image_ref.shape, jnp.float32)
    for e in range(tiles):
        vectors = ready_ref[e, :rows], None if exact else ready_ref[e, rows:]
        image += split_product(vectors, high_ref[e], low_ref[e], 0)
    image_ref[...] = image


def shift_of(devices, start_ref, sums_ref, size):
    mean = sums_ref[1, 0:1, 0:1] * (1.0 / devices)
    return mean, start_ref[size + 1, 0:1, 0:1] - mean


def first_kernel(
    devices, columns_ref, start_ref, near_ref, image_ref, total_ref, sums_ref, high_ref, low_ref,
    bundle_ref, keep_ref, products_ref,
):
    rows, order = image_ref.shape
    size = rows * order // (PAD * SIDE)
    signs = block_of(start_ref, image_ref.shape)
    image = near_ref[...] + image_ref[...] + join(total_ref[...], order // SIDE)
    image += shift_of(devices, start_ref, sums_ref, size)[1] * signs
    put(bundle_ref, 0, image)
    vectors = halves(image)
    for e in range(high_ref.shape[0]):
        products_ref[e] = split_product(vectors, high_ref[e], low_ref[e], 0)
    both = mm_t(jnp.concatenate([signs, image], axis=0), image)
    bundle_ref[size] = pack(both[:rows])
    bundle_ref[size + 1] = pack(both[rows:])
    place_products(columns_ref, products_ref, bundle_ref, keep_ref)


def root_kernel(sums_ref, start_ref, message_ref, root_ref, lines_ref):
    rows = root_ref.shape[0]
    shape = rows, lines_ref.shape[1] // 2
    root = factor(unpack(sums_ref[0], rows))[1]
    root_ref[...] = root
    lines_ref[...] = mm(root, jnp.concatenate([block_of(start_ref, shape), block_of(message_ref, shape)], axis=1))


def second_kernel(
    devices, start_ref, message_ref, near_ref, image_ref, total_ref, root_ref, lines_ref, first_sums_ref, sums_ref,
    basis_ref, result_ref, share_ref,
):
    rows, order = image_ref.shape
    mean, shift = shift_of(devices, start_ref, first_sums_ref, rows * order // (PAD * SIDE))
    root = root_ref[...]
    alpha = mm_t(mm(root, unpack(sums_ref[0], rows)), root)
    gram = mm_t(mm(root, unpack(sums_ref[1], rows)), root) - mm_t(alpha, alpha)
    image = near_ref[...] + image_ref[...] + join(total_ref[...], order // SIDE)
    image = mm(root, image + shift * block_of(message_ref, image_ref.shape))
    first_basis, first = lines_ref[:, :order], lines_ref[:, order:]
    bent = mm(alpha, lines_ref[...])
    beta, inverse = factor(gram)
    both = mm(inverse, jnp.concatenate([first - bent[:, :order], image - bent[:, order:]], axis=1))
    link = lax.dot_general(
        beta, first_basis, (((0,), (0,)), ((), ())), precision=precise, preferred_element_type=jnp.float32
    )
    basis = both[:, :order]
    result = both[:, order:] - link
    basis_ref[...] = basis
    result_ref[...] = result
    both = mm_t(jnp.concatenate([basis, result], axis=0), result)
    line = lax.broadcasted_iota(jnp.int32, (rows, rows), 0)
    lane = lax.broadcasted_iota(jnp.int32, (rows, rows), 1)
    part = 1.0 / devices
    share_ref[:, :rows] = both[:rows]
    share_ref[:, rows : 2 * rows] = both[rows:]
    share_ref[:, 2 * rows : 3 * rows] = (alpha + jnp.where(line == lane, mean, 0.0)) * part
    share_ref[:, 3 * rows :] = jnp.where(lane > line, mean, beta) * part


def last_kernel(share_ref, basis_ref, result_ref, next_ref, blocks_ref):
    rows = share_ref.shape[0]
    line = lax.broadcasted_iota(jnp.int32, (rows, rows), 0)
    lane = lax.broadcasted_iota(jnp.int32, (rows, rows), 1)
    alpha = share_ref[:, :rows]
    mean = share_ref[0:1, 4 * rows - 1 : 4 * rows]
    gram = share_ref[:, rows : 2 * rows] - mm_t(alpha, alpha)
    beta, inverse = factor(gram)
    next_ref[...] = mm(inverse, result_ref[...] - mm(alpha, basis_ref[...]))
    blocks_ref[0] = share_ref[:, 2 * rows : 3 * rows]
    blocks_ref[1] = jnp.where(lane > line, 0.0, share_ref[:, 3 * rows :])
    blocks_ref[2] = alpha + jnp.where(line == lane, mean, 0.0)
    blocks_ref[3] = beta


def call(kernel, out_shape, args, smem=0, hbm=0, scratch=(), room=8):
    args = [pltpu.with_memory_space_constraint(a, pltpu.HBM) if j < smem + hbm else a for j, a in enumerate(args)]
    outs = in_vmem if not isinstance(out_shape, tuple) else (in_vmem,) * len(out_shape)
    return pl.pallas_call(
        kernel,
        out_shape=out_shape,
        in_specs=[in_smem] * smem + [in_hbm] * hbm + [in_vmem] * (len(args) - smem - hbm),
        out_specs=outs,
        scratch_shapes=list(scratch),
        compiler_params=pltpu.CompilerParams(vmem_limit_bytes=room * 1024 * 1024),
        cost_estimate=pl.CostEstimate(flops=1, bytes_accessed=1, transcendentals=0),
    )(*args)


def body(probes, diagonal, forward_tiles, tile_columns):
    forward = forward_tiles[0]
    rows, order = probes.shape
    devices = lax.axis_size("col")

    def swapped(block, bits=1):
        return lax.ppermute(block, "col", [(i ^ bits, i) for i in range(devices)])

    def from_chips(block, *chips):
        hops = [chips[i & 1] for i in range(devices)]
        route = [((i + 2 * hops[i]) % devices, i) for i in range(devices) if hops[i] is not None]
        return lax.ppermute(block, "col", route)

    def whole(sums):
        bits = 2
        while bits < devices:
            sums = sums + swapped(sums, bits)
            bits *= 2
        return sums

    def apply(bundle, keep, near_call, exact):
        partner = swapped(bundle)
        own, its = bundle[:size], partner[:size]
        payload = bundle[size:top] + partner[size:top]
        pair = jnp.concatenate([jnp.where(lower, own, its), jnp.where(lower, its, own), payload])
        ahead = keep + partner[top:]
        near_ahead = jnp.concatenate([ahead[: 2 * size], payload])
        third_ahead = jnp.where(both_lower, pair[: 2 * size], ahead[2 * size : 4 * size])
        third_ahead = jnp.concatenate([third_ahead, payload])
        fourth_ahead = jnp.concatenate([jnp.where(lower, pair[:size], ahead[4 * size : 5 * size]), payload])
        near = from_chips(pair, 1, 2)
        near_back = from_chips(near_ahead, -1, -2)
        third = from_chips(third_ahead, 3, -3)
        fourth = from_chips(fourth_ahead, 4, -4)
        bundle, _, _ = lax.optimization_barrier((bundle, near_ahead, third_ahead))
        inner, turned = near_call(bundle)
        near, near_back, third, fourth, inner, turned = lax.optimization_barrier(
            (near, near_back, third, fourth, inner, turned)
        )
        mine = jnp.concatenate([near[: 2 * size], third[: 2 * size], fourth[:size]])
        if devices == 16:
            sums = near[2 * size :] + near_back[2 * size :] + third[2 * size :]
            sums = sums + jnp.where(lower_notes, payload + fourth[size:], 0.0)
        else:
            sums = jnp.where(lower_notes, whole(payload), 0.0)
        first = near_back[:size] + jnp.where(lower, 0.0, third[:size] + fourth[:size])
        second = near_back[size : 2 * size] + jnp.where(lower, 0.0, third[size : 2 * size] + ahead[5 * size :])
        other = jnp.concatenate([jnp.where(lower, second, first), sums])
        mine, other = lax.optimization_barrier((mine, other))
        theirs, other = swapped(mine), swapped(other)
        image = call(
            functools.partial(incoming_kernel, exact),
            struct(rows, order),
            (tile_columns, pair, mine, theirs, *turned[-2:]),
            smem=1,
            scratch=(pltpu.VMEM((tiles, 2 * rows, order), jnp.bfloat16),),
        )
        return inner, image, jnp.where(lower, first, second) + other[:size], sums + other[size:], turned

    tiles = forward.shape[0]
    size = rows * order // (PAD * SIDE)
    top = size + NOTES
    bundles = (struct(top + SLOTS * size, PAD, SIDE), struct(SLOTS * size, PAD, SIDE))
    products = pltpu.VMEM((tiles, rows, order), jnp.float32)
    split = pltpu.VMEM(forward.shape, jnp.bfloat16)
    split_diagonal = pltpu.VMEM(diagonal.shape, jnp.bfloat16)
    start, core, keep, high, low = call(
        begin_kernel,
        (bundles[0], pltpu.VMEM((size, PAD, SIDE), jnp.int32), bundles[1], split, split),
        (tile_columns, probes, diagonal, forward),
        smem=1,
        hbm=3,
        room=12,
        scratch=(
            pltpu.VMEM(probes.shape, jnp.int32),
            pltpu.VMEM((order // SIDE, SIDE, SIDE), jnp.float32),
            pltpu.VMEM(forward.shape, jnp.float32),
            products,
            pltpu.SemaphoreType.DMA((tiles + 1 + order // SIDE,)),
        ),
    )
    lower = core == 0
    lower_notes = lower[:NOTES]
    both_lower = jnp.concatenate([lower, lower])

    def first_near(bundle):
        made = call(
            first_near_kernel,
            (struct(rows, order), split_diagonal, split_diagonal, split, split),
            (bundle, diagonal, high, low),
        )
        return made[0], made[1:]

    inner, image, total, start_sums, turned = apply(start, keep, first_near, True)
    diagonal_high, diagonal_low, *turned = turned
    message, keep = call(
        functools.partial(first_kernel, devices),
        bundles,
        (tile_columns, start, inner, image, total, start_sums, high, low),
        smem=1,
        scratch=(products,),
    )
    def second_near(bundle):
        inner = call(second_near_kernel, struct(rows, order), (bundle, diagonal_high, diagonal_low))
        ahead = call(root_kernel, (struct(rows, rows), struct(rows, 2 * order)), (start_sums, start, bundle))
        return inner, (*ahead, *turned)

    inner, image, total, sums, (root, lines, *_) = apply(message, keep, second_near, False)
    basis, result, share = call(
        functools.partial(second_kernel, devices),
        (struct(rows, order), struct(rows, order), struct(rows, SIDE)),
        (start, message, inner, image, total, root, lines, start_sums, sums),
    )
    bits = 1
    while bits < devices:
        if 4 * bits <= devices:
            one, two, three = (swapped(share, bits * j) for j in (1, 2, 3))
            share = (share + one) + (two + three)
            bits *= 4
        else:
            share = share + swapped(share, bits)
            bits *= 2
    outs = (jax.ShapeDtypeStruct((rows, order), jnp.float32), jax.ShapeDtypeStruct((4, rows, rows), jnp.float32))
    return call(last_kernel, outs, (share, basis, result))


def solution(mesh):
    placed = (
        P(None, ("groups", "col")),
        P(("groups", "col"), None),
        P(("groups", "col"), None, None, None),
        P(("groups", "col"), None),
    )
    return jax.shard_map(
        body,
        mesh=mesh,
        in_specs=placed,
        out_specs=(P(None, ("groups", "col")), P("groups", None, None)),
        check_vma=False,
    )
```

```python
import functools

import jax
import jax.numpy as jnp
from jax import lax
from jax.experimental import pallas as pl
from jax.experimental.pallas import tpu as pltpu
from jax.sharding import PartitionSpec as P

SCALE = 0.0078125
SIDE = 128
PAD = 8
SLOTS = 6

precise = lax.Precision.HIGHEST
in_vmem = pl.BlockSpec(memory_space=pltpu.VMEM)
in_hbm = pl.BlockSpec(memory_space=pltpu.HBM)
in_smem = pl.BlockSpec(memory_space=pltpu.SMEM)


def struct(*shape):
    return pltpu.VMEM(shape, jnp.float32)


def mm(left, right):
    return lax.dot_general(
        left, right, (((1,), (0,)), ((), ())), precision=precise, preferred_element_type=jnp.float32
    )


def mm_t(left, right):
    return lax.dot_general(
        left, right, (((1,), (1,)), ((), ())), precision=precise, preferred_element_type=jnp.float32
    )


def halves(block):
    high = block.astype(jnp.bfloat16)
    return high, (block - high.astype(jnp.float32)).astype(jnp.bfloat16)


def split_product(vectors, matrix_high, matrix_low, side):
    dims = (((1,), (side,)), ((), ()))
    dot = functools.partial(lax.dot_general, dimension_numbers=dims, preferred_element_type=jnp.float32)
    high, low = vectors
    if low is None:
        return dot(high, matrix_high) + dot(high, matrix_low)
    rows = high.shape[0]
    both = dot(jnp.concatenate([high, low], axis=0), matrix_high)
    return both[:rows] + both[rows:] + dot(high, matrix_low)


def parts_of(block, exact):
    if exact:
        return block.astype(jnp.bfloat16), None
    return halves(block)


def factor(matrix):
    size = matrix.shape[0]
    step = 8
    strips = size // step
    lane = lax.broadcasted_iota(jnp.int32, (step, size), 1)
    rows = [lax.broadcasted_iota(jnp.int32, (step, size), 0) + step * s for s in range(strips)]
    columns = [
        [jnp.broadcast_to(matrix[step * s : step * s + step, j : j + 1], (step, size)) for s in range(strips)]
        for j in range(size)
    ]
    inverse = [jnp.where(lane == rows[s], 1.0, 0.0) for s in range(strips)]
    lower = [jnp.zeros((step, size), jnp.float32) for _ in range(strips)]
    for k in range(size):
        home, at = divmod(k, step)
        pivot = jnp.broadcast_to(columns[k][home][at : at + 1, :], (step, size))
        root = lax.rsqrt(pivot)
        root = root * (1.5 - 0.5 * (pivot * root) * root)
        scaled = [None] * strips
        for s in range(home, strips):
            scaled[s] = columns[k][s] * root
            if s == home:
                scaled[s] = jnp.where(rows[s] >= k, scaled[s], 0.0)
            lower[s] = jnp.where(lane == k, scaled[s], lower[s])
        for j in range(k + 1, size):
            place, inside = divmod(j, step)
            weight = jnp.broadcast_to(scaled[place][inside : inside + 1, :], (step, size))
            for s in range(place, strips):
                columns[j][s] = columns[j][s] - scaled[s] * weight
        done = jnp.broadcast_to(inverse[home][at : at + 1, :], (step, size)) * root
        for s in range(home, strips):
            if s == home:
                inverse[s] = jnp.where(rows[s] == k, done, inverse[s] - jnp.where(rows[s] > k, scaled[s], 0.0) * done)
            else:
                inverse[s] = inverse[s] - scaled[s] * done
    return jnp.concatenate(lower, axis=0), jnp.concatenate(inverse, axis=0)


def pack(matrix):
    return jnp.concatenate([matrix[q : q + PAD] for q in range(0, matrix.shape[0], PAD)], axis=1)


def unpack(tile, side):
    return jnp.concatenate([tile[:, q : q + side] for q in range(0, SIDE, side)], axis=0)


def join(tiles, wide):
    rows = [jnp.concatenate([tiles[q + j] for j in range(wide)], axis=1) for q in range(0, tiles.shape[0], wide)]
    return jnp.concatenate(rows, axis=0)


def put(ref, base, block):
    wide = block.shape[1] // SIDE
    for i in range(block.shape[0] // PAD):
        for j in range(wide):
            ref[base + wide * i + j] = block[PAD * i : PAD * i + PAD, SIDE * j : SIDE * j + SIDE]


def block_of(ref, shape):
    rows, order = shape
    return join(ref[: rows * order // (PAD * SIDE)], order // SIDE)


def diagonal_of(side):
    return lax.broadcasted_iota(jnp.int32, (side, side), 0) == lax.broadcasted_iota(jnp.int32, (side, side), 1)


def place_of(columns_ref, e):
    devices = lax.axis_size("col")
    position = lax.axis_index("col")
    core = position & 1
    ahead = core + lax.rem(columns_ref[0, e] - position + devices, devices)
    return core, ahead >> 1, ahead & 1


def place_products(columns_ref, products_ref, bundle_ref, keep_ref):
    size = keep_ref.shape[0] // SLOTS
    start = bundle_ref.shape[0] - keep_ref.shape[0]
    keep_ref[...] = jnp.zeros_like(keep_ref)
    bundle_ref[start:] = jnp.zeros_like(keep_ref)
    for e in range(products_ref.shape[0]):
        core, chip, block = place_of(columns_ref, e)
        speaker = jnp.where(chip == 1, 0, 1)
        slot = jnp.where(chip == 0, SLOTS - 1, jnp.where(chip < 3, 0, 2 * chip - 4) + block)

        @pl.when(speaker == core)
        def _():
            put(keep_ref, slot * size, products_ref[e])

        @pl.when(speaker != core)
        def _():
            put(bundle_ref, start + slot * size, products_ref[e])


def begin_kernel(
    columns_ref, probes_hbm, diagonal_hbm, forward_hbm,
    bundle_ref, core_ref, keep_ref, high_ref, low_ref,
    probes_ref, diagonal_ref, forward_ref, products_ref, sems,
):
    tiles = forward_ref.shape[0]
    squares = diagonal_ref.shape[0]
    copies = [pltpu.make_async_copy(probes_hbm, probes_ref, sems.at[0])]
    for q in range(squares):
        ends = pl.ds(SIDE * q, SIDE)
        copies += [pltpu.make_async_copy(diagonal_hbm.at[ends, ends], diagonal_ref.at[q], sems.at[1 + q])]
    for e in range(tiles):
        copies += [pltpu.make_async_copy(forward_hbm.at[e], forward_ref.at[e], sems.at[1 + squares + e])]
    for copy in copies:
        copy.start()
    core_ref[...] = jnp.full(core_ref.shape, lax.axis_index("col") & 1, jnp.int32)
    copies[0].wait()
    signs = (2 * probes_ref[...] - 1).astype(jnp.float32) * SCALE
    rows, order = signs.shape
    size = rows * order // (PAD * SIDE)
    put(bundle_ref, 0, signs)
    square = lax.broadcasted_iota(jnp.int32, (SIDE, SIDE), 0) == lax.broadcasted_iota(jnp.int32, (SIDE, SIDE), 1)
    trace = jnp.zeros((SIDE, SIDE), jnp.float32)
    for q in range(squares):
        copies[1 + q].wait()
        trace += jnp.where(square, diagonal_ref[q], 0.0) * (1.0 / order)
    trace = jnp.sum(jnp.sum(trace, axis=0, keepdims=True), axis=1, keepdims=True)
    bundle_ref[size] = pack(jnp.where(diagonal_of(rows), trace, mm_t(signs, signs)))
    exact = (signs.astype(jnp.bfloat16), None)
    for e in range(tiles):
        copies[1 + squares + e].wait()
        high, low = halves(forward_ref[e])
        high_ref[e] = high
        low_ref[e] = low
        products_ref[e] = split_product(exact, high, low, 0)
    place_products(columns_ref, products_ref, bundle_ref, keep_ref)


def first_near_kernel(
    bundle_ref, diagonal_ref, tile_high_ref, tile_low_ref, image_ref, high_ref, low_ref, turned_high_ref, turned_low_ref
):
    rows, order = image_ref.shape
    trace = bundle_ref[rows * order // (PAD * SIDE), 0:1, 0:1]
    line = lax.broadcasted_iota(jnp.int32, (order, order), 0) == lax.broadcasted_iota(jnp.int32, (order, order), 1)
    high, low = halves(diagonal_ref[...] - jnp.where(line, trace, 0.0))
    high_ref[...] = high
    low_ref[...] = low
    image_ref[...] = split_product(parts_of(block_of(bundle_ref, image_ref.shape), True), high, low, 0)
    for e in range(tile_high_ref.shape[0]):
        turned_high_ref[e] = tile_high_ref[e].T
        turned_low_ref[e] = tile_low_ref[e].T


def second_near_kernel(bundle_ref, high_ref, low_ref, image_ref):
    image_ref[...] = split_product(parts_of(block_of(bundle_ref, image_ref.shape), False), high_ref[...], low_ref[...], 0)


def incoming(shape, exact, columns_ref, pair_ref, mine_ref, theirs_ref, high_ref, low_ref, ready_ref):
    rows, order = shape
    size = rows * order // (PAD * SIDE)
    tiles = high_ref.shape[0]
    for e in range(tiles):
        core, chip, block = place_of(columns_ref, e)
        speaker = jnp.where(chip == 2, 1, 0)
        part = jnp.where(chip < 3, 0, 2 * chip - 4)
        met = jnp.where(
            speaker == core, mine_ref[pl.ds((part + block) * size, size)], theirs_ref[pl.ds((part + block) * size, size)]
        )
        met = join(jnp.where(chip == 0, pair_ref[pl.ds(block * size, size)], met), order // SIDE)
        high, low = parts_of(met, exact)
        ready_ref[e, :rows] = high
        if not exact:
            ready_ref[e, rows:] = low
    image = jnp.zeros(shape, jnp.float32)
    for e in range(tiles):
        vectors = ready_ref[e, :rows], None if exact else ready_ref[e, rows:]
        image += split_product(vectors, high_ref[e], low_ref[e], 0)
    return image


def shift_of(devices, start_ref, sums_ref, size):
    mean = sums_ref[0, 0:1, 0:1] * (1.0 / devices)
    return mean, start_ref[size, 0:1, 0:1] - mean


def first_kernel(
    devices, columns_ref, start_ref, near_ref, total_ref, sums_ref, high_ref, low_ref,
    pair_ref, mine_ref, theirs_ref, turned_high_ref, turned_low_ref,
    bundle_ref, keep_ref, products_ref, ready_ref,
):
    rows, order = near_ref.shape
    size = rows * order // (PAD * SIDE)
    signs = block_of(start_ref, near_ref.shape)
    image = incoming(
        near_ref.shape, True, columns_ref, pair_ref, mine_ref, theirs_ref, turned_high_ref, turned_low_ref, ready_ref
    )
    image += near_ref[...] + join(total_ref[...], order // SIDE)
    image += shift_of(devices, start_ref, sums_ref, size)[1] * signs
    put(bundle_ref, 0, image)
    vectors = halves(image)
    for e in range(high_ref.shape[0]):
        products_ref[e] = split_product(vectors, high_ref[e], low_ref[e], 0)
    both = mm_t(jnp.concatenate([signs, image], axis=0), image)
    bundle_ref[size] = pack(both[:rows])
    bundle_ref[size + 1] = pack(both[rows:])
    place_products(columns_ref, products_ref, bundle_ref, keep_ref)


def root_kernel(devices, sums_ref, start_ref, message_ref, root_ref, lines_ref):
    rows = root_ref.shape[0]
    shape = rows, lines_ref.shape[1] // 2
    square = devices * shape[1] * SCALE * SCALE
    root = factor(jnp.where(diagonal_of(rows), square, unpack(sums_ref[0], rows)))[1]
    root_ref[...] = root
    lines_ref[...] = mm(root, jnp.concatenate([block_of(start_ref, shape), block_of(message_ref, shape)], axis=1))


def second_kernel(
    devices, columns_ref, start_ref, message_ref, near_ref, total_ref, root_ref, lines_ref, first_sums_ref, sums_ref,
    pair_ref, mine_ref, theirs_ref, turned_high_ref, turned_low_ref,
    basis_ref, result_ref, share_ref, ready_ref,
):
    rows, order = near_ref.shape
    mean, shift = shift_of(devices, start_ref, first_sums_ref, rows * order // (PAD * SIDE))
    root = root_ref[...]
    alpha = mm_t(mm(root, unpack(sums_ref[0], rows)), root)
    gram = mm_t(mm(root, unpack(sums_ref[1], rows)), root) - mm_t(alpha, alpha)
    image = incoming(
        near_ref.shape, False, columns_ref, pair_ref, mine_ref, theirs_ref, turned_high_ref, turned_low_ref, ready_ref
    )
    image += near_ref[...] + join(total_ref[...], order // SIDE)
    image = mm(root, image + shift * block_of(message_ref, near_ref.shape))
    first_basis, first = lines_ref[:, :order], lines_ref[:, order:]
    bent = mm(alpha, lines_ref[...])
    beta, inverse = factor(gram)
    both = mm(inverse, jnp.concatenate([first - bent[:, :order], image - bent[:, order:]], axis=1))
    link = lax.dot_general(
        beta, first_basis, (((0,), (0,)), ((), ())), precision=precise, preferred_element_type=jnp.float32
    )
    basis = both[:, :order]
    result = both[:, order:] - link
    basis_ref[...] = basis
    result_ref[...] = result
    both = mm_t(jnp.concatenate([basis, result], axis=0), result)
    line = lax.broadcasted_iota(jnp.int32, (rows, rows), 0)
    lane = lax.broadcasted_iota(jnp.int32, (rows, rows), 1)
    part = 1.0 / devices
    share_ref[:, :rows] = both[:rows]
    share_ref[:, rows : 2 * rows] = both[rows:]
    share_ref[:, 2 * rows : 3 * rows] = (alpha + jnp.where(line == lane, mean, 0.0)) * part
    share_ref[:, 3 * rows :] = jnp.where(lane > line, mean, beta) * part


def last_kernel(share_ref, basis_ref, result_ref, next_ref, blocks_ref):
    rows = share_ref.shape[0]
    line = lax.broadcasted_iota(jnp.int32, (rows, rows), 0)
    lane = lax.broadcasted_iota(jnp.int32, (rows, rows), 1)
    alpha = share_ref[:, :rows]
    mean = share_ref[0:1, 4 * rows - 1 : 4 * rows]
    gram = share_ref[:, rows : 2 * rows] - mm_t(alpha, alpha)
    beta, inverse = factor(gram)
    next_ref[...] = mm(inverse, result_ref[...] - mm(alpha, basis_ref[...]))
    blocks_ref[0] = share_ref[:, 2 * rows : 3 * rows]
    blocks_ref[1] = jnp.where(lane > line, 0.0, share_ref[:, 3 * rows :])
    blocks_ref[2] = alpha + jnp.where(line == lane, mean, 0.0)
    blocks_ref[3] = beta


def call(kernel, out_shape, args, smem=0, hbm=0, scratch=(), room=8):
    args = [pltpu.with_memory_space_constraint(a, pltpu.HBM) if j < smem + hbm else a for j, a in enumerate(args)]
    outs = in_vmem if not isinstance(out_shape, tuple) else (in_vmem,) * len(out_shape)
    return pl.pallas_call(
        kernel,
        out_shape=out_shape,
        in_specs=[in_smem] * smem + [in_hbm] * hbm + [in_vmem] * (len(args) - smem - hbm),
        out_specs=outs,
        scratch_shapes=list(scratch),
        compiler_params=pltpu.CompilerParams(vmem_limit_bytes=room * 1024 * 1024),
        cost_estimate=pl.CostEstimate(flops=1, bytes_accessed=1, transcendentals=0),
    )(*args)


def body(probes, diagonal, forward_tiles, tile_columns):
    forward = forward_tiles[0]
    rows, order = probes.shape
    devices = lax.axis_size("col")

    def swapped(block, bits=1):
        return lax.ppermute(block, "col", [(i ^ bits, i) for i in range(devices)])

    def from_chips(block, *chips):
        hops = [chips[i & 1] for i in range(devices)]
        route = [((i + 2 * hops[i]) % devices, i) for i in range(devices) if hops[i] is not None]
        return lax.ppermute(block, "col", route)

    def whole(sums):
        bits = 2
        while bits < devices:
            sums = sums + swapped(sums, bits)
            bits *= 2
        return sums

    def apply(bundle, keep, near_call):
        top = bundle.shape[0] - keep.shape[0]
        partner = swapped(bundle)
        own, its = bundle[:size], partner[:size]
        payload = bundle[size:top] + partner[size:top]
        pair = jnp.concatenate([jnp.where(lower, own, its), jnp.where(lower, its, own), payload])
        ahead = keep + partner[top:]
        near_ahead = jnp.concatenate([ahead[: 2 * size], payload])
        third_ahead = jnp.where(both_lower, pair[: 2 * size], ahead[2 * size : 4 * size])
        third_ahead = jnp.concatenate([third_ahead, payload])
        fourth_ahead = jnp.concatenate([jnp.where(lower, pair[:size], ahead[4 * size : 5 * size]), payload])
        near = from_chips(pair, 1, 2)
        near_back = from_chips(near_ahead, -1, -2)
        third = from_chips(third_ahead, 3, -3)
        fourth = from_chips(fourth_ahead, 4, -4)
        bundle, _, _ = lax.optimization_barrier((bundle, near_ahead, third_ahead))
        inner, turned = near_call(bundle)
        near, near_back, third, fourth, inner, turned = lax.optimization_barrier(
            (near, near_back, third, fourth, inner, turned)
        )
        mine = jnp.concatenate([near[: 2 * size], third[: 2 * size], fourth[:size]])
        if devices == 16:
            sums = near[2 * size :] + near_back[2 * size :] + third[2 * size :]
            sums = sums + jnp.where(lower[: top - size], payload + fourth[size:], 0.0)
        else:
            sums = jnp.where(lower[: top - size], whole(payload), 0.0)
        first = near_back[:size] + jnp.where(lower, 0.0, third[:size] + fourth[:size])
        second = near_back[size : 2 * size] + jnp.where(lower, 0.0, third[size : 2 * size] + ahead[5 * size :])
        other = jnp.concatenate([jnp.where(lower, second, first), sums])
        mine, other = lax.optimization_barrier((mine, other))
        theirs, other = swapped(mine), swapped(other)
        total = jnp.where(lower, first, second) + other[:size]
        return inner, total, sums + other[size:], (pair, mine, theirs), turned

    tiles = forward.shape[0]
    size = rows * order // (PAD * SIDE)
    slots = struct(SLOTS * size, PAD, SIDE)
    bundles = [struct(size + notes + SLOTS * size, PAD, SIDE) for notes in (1, 2)]
    products = pltpu.VMEM((tiles, rows, order), jnp.float32)
    split = pltpu.VMEM(forward.shape, jnp.bfloat16)
    split_diagonal = pltpu.VMEM(diagonal.shape, jnp.bfloat16)
    start, core, keep, high, low = call(
        begin_kernel,
        (bundles[0], pltpu.VMEM((size, PAD, SIDE), jnp.int32), slots, split, split),
        (tile_columns, probes, diagonal, forward),
        smem=1,
        hbm=3,
        room=12,
        scratch=(
            pltpu.VMEM(probes.shape, jnp.int32),
            pltpu.VMEM((order // SIDE, SIDE, SIDE), jnp.float32),
            pltpu.VMEM(forward.shape, jnp.float32),
            products,
            pltpu.SemaphoreType.DMA((tiles + 1 + order // SIDE,)),
        ),
    )
    lower = core == 0
    both_lower = jnp.concatenate([lower, lower])

    def first_near(bundle):
        made = call(
            first_near_kernel,
            (struct(rows, order), split_diagonal, split_diagonal, split, split),
            (bundle, diagonal, high, low),
        )
        return made[0], made[1:]

    inner, total, start_sums, met, turned = apply(start, keep, first_near)
    diagonal_high, diagonal_low, *turned = turned
    ready = pltpu.VMEM((tiles, 2 * rows, order), jnp.bfloat16)
    message, keep = call(
        functools.partial(first_kernel, devices),
        (bundles[1], slots),
        (tile_columns, start, inner, total, start_sums, high, low, *met, *turned),
        smem=1,
        scratch=(products, ready),
    )

    def second_near(bundle):
        inner = call(second_near_kernel, struct(rows, order), (bundle, diagonal_high, diagonal_low))
        ahead = call(
            functools.partial(root_kernel, devices),
            (struct(rows, rows), struct(rows, 2 * order)),
            (start_sums, start, bundle),
        )
        return inner, ahead

    inner, total, sums, met, (root, lines) = apply(message, keep, second_near)
    basis, result, share = call(
        functools.partial(second_kernel, devices),
        (struct(rows, order), struct(rows, order), struct(rows, SIDE)),
        (tile_columns, start, message, inner, total, root, lines, start_sums, sums, *met, *turned),
        smem=1,
        scratch=(ready,),
    )
    bits = 1
    while bits < devices:
        if 4 * bits <= devices:
            one, two, three = (swapped(share, bits * j) for j in (1, 2, 3))
            share = (share + one) + (two + three)
            bits *= 4
        else:
            share = share + swapped(share, bits)
            bits *= 2
    outs = (jax.ShapeDtypeStruct((rows, order), jnp.float32), jax.ShapeDtypeStruct((4, rows, rows), jnp.float32))
    return call(last_kernel, outs, (share, basis, result))


def solution(mesh):
    placed = (
        P(None, ("groups", "col")),
        P(("groups", "col"), None),
        P(("groups", "col"), None, None, None),
        P(("groups", "col"), None),
    )
    return jax.shard_map(
        body,
        mesh=mesh,
        in_specs=placed,
        out_specs=(P(None, ("groups", "col")), P("groups", None, None)),
        check_vma=False,
    )
```

```python
import functools

import jax
import jax.numpy as jnp
from jax import lax
from jax.experimental import pallas as pl
from jax.experimental.pallas import tpu as pltpu
from jax.sharding import PartitionSpec as P

SCALE = 0.0078125
SIDE = 128
PAD = 8
SLOTS = 6

precise = lax.Precision.HIGHEST
in_vmem = pl.BlockSpec(memory_space=pltpu.VMEM)
in_hbm = pl.BlockSpec(memory_space=pltpu.HBM)
in_smem = pl.BlockSpec(memory_space=pltpu.SMEM)


def struct(*shape):
    return pltpu.VMEM(shape, jnp.float32)


def mm(left, right):
    return lax.dot_general(
        left, right, (((1,), (0,)), ((), ())), precision=precise, preferred_element_type=jnp.float32
    )


def mm_t(left, right):
    return lax.dot_general(
        left, right, (((1,), (1,)), ((), ())), precision=precise, preferred_element_type=jnp.float32
    )


def halves(block):
    high = block.astype(jnp.bfloat16)
    return high, (block - high.astype(jnp.float32)).astype(jnp.bfloat16)


def split_product(vectors, matrix_high, matrix_low, side):
    dims = (((1,), (side,)), ((), ()))
    dot = functools.partial(lax.dot_general, dimension_numbers=dims, preferred_element_type=jnp.float32)
    high, low = vectors
    if low is None:
        return dot(high, matrix_high) + dot(high, matrix_low)
    rows = high.shape[0]
    both = dot(jnp.concatenate([high, low], axis=0), matrix_high)
    return both[:rows] + both[rows:] + dot(high, matrix_low)


def parts_of(block, exact):
    if exact:
        return block.astype(jnp.bfloat16), None
    return halves(block)


def factor(matrix):
    size = matrix.shape[0]
    step = 8
    strips = size // step
    lane = lax.broadcasted_iota(jnp.int32, (step, size), 1)
    rows = [lax.broadcasted_iota(jnp.int32, (step, size), 0) + step * s for s in range(strips)]
    columns = [
        [jnp.broadcast_to(matrix[step * s : step * s + step, j : j + 1], (step, size)) for s in range(strips)]
        for j in range(size)
    ]
    inverse = [jnp.where(lane == rows[s], 1.0, 0.0) for s in range(strips)]
    lower = [jnp.zeros((step, size), jnp.float32) for _ in range(strips)]
    for k in range(size):
        home, at = divmod(k, step)
        pivot = jnp.broadcast_to(columns[k][home][at : at + 1, :], (step, size))
        root = lax.rsqrt(pivot)
        root = root * (1.5 - 0.5 * (pivot * root) * root)
        scaled = [None] * strips
        for s in range(home, strips):
            scaled[s] = columns[k][s] * root
            if s == home:
                scaled[s] = jnp.where(rows[s] >= k, scaled[s], 0.0)
            lower[s] = jnp.where(lane == k, scaled[s], lower[s])
        for j in range(k + 1, size):
            place, inside = divmod(j, step)
            weight = jnp.broadcast_to(scaled[place][inside : inside + 1, :], (step, size))
            for s in range(place, strips):
                columns[j][s] = columns[j][s] - scaled[s] * weight
        done = jnp.broadcast_to(inverse[home][at : at + 1, :], (step, size)) * root
        for s in range(home, strips):
            if s == home:
                inverse[s] = jnp.where(rows[s] == k, done, inverse[s] - jnp.where(rows[s] > k, scaled[s], 0.0) * done)
            else:
                inverse[s] = inverse[s] - scaled[s] * done
    return jnp.concatenate(lower, axis=0), jnp.concatenate(inverse, axis=0)


def pack(matrix):
    return jnp.concatenate([matrix[q : q + PAD] for q in range(0, matrix.shape[0], PAD)], axis=1)


def unpack(tile, side):
    return jnp.concatenate([tile[:, q : q + side] for q in range(0, SIDE, side)], axis=0)


def join(tiles, wide):
    rows = [jnp.concatenate([tiles[q + j] for j in range(wide)], axis=1) for q in range(0, tiles.shape[0], wide)]
    return jnp.concatenate(rows, axis=0)


def put(ref, base, block):
    wide = block.shape[1] // SIDE
    for i in range(block.shape[0] // PAD):
        for j in range(wide):
            ref[base + wide * i + j] = block[PAD * i : PAD * i + PAD, SIDE * j : SIDE * j + SIDE]


def block_of(ref, shape):
    rows, order = shape
    return join(ref[: rows * order // (PAD * SIDE)], order // SIDE)


def diagonal_of(side):
    return lax.broadcasted_iota(jnp.int32, (side, side), 0) == lax.broadcasted_iota(jnp.int32, (side, side), 1)


def place_of(columns_ref, e):
    devices = lax.axis_size("col")
    position = lax.axis_index("col")
    core = position & 1
    ahead = core + lax.rem(columns_ref[0, e] - position + devices, devices)
    return core, ahead >> 1, ahead & 1


def place_products(columns_ref, products_ref, bundle_ref, keep_ref):
    size = keep_ref.shape[0] // SLOTS
    start = bundle_ref.shape[0] - keep_ref.shape[0]
    keep_ref[...] = jnp.zeros_like(keep_ref)
    bundle_ref[start:] = jnp.zeros_like(keep_ref)
    for e in range(products_ref.shape[0]):
        core, chip, block = place_of(columns_ref, e)
        speaker = jnp.where(chip == 1, 0, 1)
        slot = jnp.where(chip == 0, SLOTS - 1, jnp.where(chip < 3, 0, 2 * chip - 4) + block)

        @pl.when(speaker == core)
        def _():
            put(keep_ref, slot * size, products_ref[e])

        @pl.when(speaker != core)
        def _():
            put(bundle_ref, start + slot * size, products_ref[e])


def begin_kernel(
    columns_ref, probes_hbm, diagonal_hbm, forward_hbm,
    bundle_ref, core_ref, keep_ref, high_ref, low_ref,
    probes_ref, diagonal_ref, forward_ref, products_ref, sems,
):
    tiles = forward_ref.shape[0]
    squares = diagonal_ref.shape[0]
    copies = [pltpu.make_async_copy(probes_hbm, probes_ref, sems.at[0])]
    for q in range(squares):
        ends = pl.ds(SIDE * q, SIDE)
        copies += [pltpu.make_async_copy(diagonal_hbm.at[ends, ends], diagonal_ref.at[q], sems.at[1 + q])]
    for e in range(tiles):
        copies += [pltpu.make_async_copy(forward_hbm.at[e], forward_ref.at[e], sems.at[1 + squares + e])]
    for copy in copies:
        copy.start()
    core_ref[...] = jnp.full(core_ref.shape, lax.axis_index("col") & 1, jnp.int32)
    copies[0].wait()
    signs = (2 * probes_ref[...] - 1).astype(jnp.float32) * SCALE
    rows, order = signs.shape
    size = rows * order // (PAD * SIDE)
    put(bundle_ref, 0, signs)
    square = lax.broadcasted_iota(jnp.int32, (SIDE, SIDE), 0) == lax.broadcasted_iota(jnp.int32, (SIDE, SIDE), 1)
    trace = jnp.zeros((SIDE, SIDE), jnp.float32)
    for q in range(squares):
        copies[1 + q].wait()
        trace += jnp.where(square, diagonal_ref[q], 0.0) * (1.0 / order)
    trace = jnp.sum(jnp.sum(trace, axis=0, keepdims=True), axis=1, keepdims=True)
    bundle_ref[size] = pack(jnp.where(diagonal_of(rows), trace, mm_t(signs, signs)))
    exact = (signs.astype(jnp.bfloat16), None)
    for e in range(tiles):
        copies[1 + squares + e].wait()
        high, low = halves(forward_ref[e])
        high_ref[e] = high
        low_ref[e] = low
        products_ref[e] = split_product(exact, high, low, 0)
    place_products(columns_ref, products_ref, bundle_ref, keep_ref)


def first_near_kernel(
    bundle_ref, diagonal_ref, tile_high_ref, tile_low_ref, image_ref, high_ref, low_ref, turned_high_ref, turned_low_ref
):
    rows, order = image_ref.shape
    trace = bundle_ref[rows * order // (PAD * SIDE), 0:1, 0:1]
    line = lax.broadcasted_iota(jnp.int32, (order, order), 0) == lax.broadcasted_iota(jnp.int32, (order, order), 1)
    high, low = halves(diagonal_ref[...] - jnp.where(line, trace, 0.0))
    high_ref[...] = high
    low_ref[...] = low
    image_ref[...] = split_product(parts_of(block_of(bundle_ref, image_ref.shape), True), high, low, 0)
    for e in range(tile_high_ref.shape[0]):
        turned_high_ref[e] = tile_high_ref[e].T
        turned_low_ref[e] = tile_low_ref[e].T


def second_near_kernel(bundle_ref, high_ref, low_ref, image_ref):
    image_ref[...] = split_product(parts_of(block_of(bundle_ref, image_ref.shape), False), high_ref[...], low_ref[...], 0)


def incoming(shape, exact, columns_ref, pair_ref, mine_ref, theirs_ref, high_ref, low_ref, ready_ref):
    rows, order = shape
    size = rows * order // (PAD * SIDE)
    tiles = high_ref.shape[0]
    for e in range(tiles):
        core, chip, block = place_of(columns_ref, e)
        speaker = jnp.where(chip == 2, 1, 0)
        part = jnp.where(chip < 3, 0, 2 * chip - 4)
        met = jnp.where(
            speaker == core, mine_ref[pl.ds((part + block) * size, size)], theirs_ref[pl.ds((part + block) * size, size)]
        )
        met = join(jnp.where(chip == 0, pair_ref[pl.ds(block * size, size)], met), order // SIDE)
        high, low = parts_of(met, exact)
        ready_ref[e, :rows] = high
        if not exact:
            ready_ref[e, rows:] = low
    image = jnp.zeros(shape, jnp.float32)
    for e in range(tiles):
        vectors = ready_ref[e, :rows], None if exact else ready_ref[e, rows:]
        image += split_product(vectors, high_ref[e], low_ref[e], 0)
    return image


def shift_of(devices, start_ref, sums_ref, size):
    mean = sums_ref[0, 0:1, 0:1] * (1.0 / devices)
    return mean, start_ref[size, 0:1, 0:1] - mean


def first_kernel(
    devices, columns_ref, start_ref, near_ref, total_ref, sums_ref, high_ref, low_ref,
    pair_ref, mine_ref, theirs_ref, turned_high_ref, turned_low_ref,
    bundle_ref, keep_ref, products_ref, ready_ref,
):
    rows, order = near_ref.shape
    size = rows * order // (PAD * SIDE)
    signs = block_of(start_ref, near_ref.shape)
    image = incoming(
        near_ref.shape, True, columns_ref, pair_ref, mine_ref, theirs_ref, turned_high_ref, turned_low_ref, ready_ref
    )
    image += near_ref[...] + join(total_ref[...], order // SIDE)
    image += shift_of(devices, start_ref, sums_ref, size)[1] * signs
    put(bundle_ref, 0, image)
    vectors = halves(image)
    for e in range(high_ref.shape[0]):
        products_ref[e] = split_product(vectors, high_ref[e], low_ref[e], 0)
    both = mm_t(jnp.concatenate([signs, image], axis=0), image)
    bundle_ref[size] = pack(both[:rows])
    bundle_ref[size + 1] = pack(both[rows:])
    place_products(columns_ref, products_ref, bundle_ref, keep_ref)


def root_kernel(devices, sums_ref, start_ref, message_ref, root_ref, lines_ref):
    rows = root_ref.shape[0]
    shape = rows, lines_ref.shape[1] // 2
    square = devices * shape[1] * SCALE * SCALE
    root = factor(jnp.where(diagonal_of(rows), square, unpack(sums_ref[0], rows)))[1]
    root_ref[...] = root
    lines_ref[...] = mm(root, jnp.concatenate([block_of(start_ref, shape), block_of(message_ref, shape)], axis=1))


def second_kernel(
    devices, columns_ref, start_ref, message_ref, near_ref, total_ref, root_ref, lines_ref, first_sums_ref, sums_ref,
    pair_ref, mine_ref, theirs_ref, turned_high_ref, turned_low_ref,
    basis_ref, result_ref, share_ref, ready_ref,
):
    rows, order = near_ref.shape
    mean, shift = shift_of(devices, start_ref, first_sums_ref, rows * order // (PAD * SIDE))
    root = root_ref[...]
    alpha = mm_t(mm(root, unpack(sums_ref[0], rows)), root)
    gram = mm_t(mm(root, unpack(sums_ref[1], rows)), root) - mm_t(alpha, alpha)
    image = incoming(
        near_ref.shape, False, columns_ref, pair_ref, mine_ref, theirs_ref, turned_high_ref, turned_low_ref, ready_ref
    )
    image += near_ref[...] + join(total_ref[...], order // SIDE)
    image = mm(root, image + shift * block_of(message_ref, near_ref.shape))
    first_basis, first = lines_ref[:, :order], lines_ref[:, order:]
    bent = mm(alpha, lines_ref[...])
    beta, inverse = factor(gram)
    both = mm(inverse, jnp.concatenate([first - bent[:, :order], image - bent[:, order:]], axis=1))
    link = lax.dot_general(
        beta, first_basis, (((0,), (0,)), ((), ())), precision=precise, preferred_element_type=jnp.float32
    )
    basis = both[:, :order]
    result = both[:, order:] - link
    basis_ref[...] = basis
    result_ref[...] = result
    both = mm_t(jnp.concatenate([basis, result], axis=0), result)
    line = lax.broadcasted_iota(jnp.int32, (rows, rows), 0)
    lane = lax.broadcasted_iota(jnp.int32, (rows, rows), 1)
    part = 1.0 / devices
    share_ref[:, :rows] = both[:rows]
    share_ref[:, rows : 2 * rows] = both[rows:]
    share_ref[:, 2 * rows : 3 * rows] = (alpha + jnp.where(line == lane, mean, 0.0)) * part
    share_ref[:, 3 * rows :] = jnp.where(lane > line, mean, beta) * part


def last_kernel(share_ref, basis_ref, result_ref, next_ref, blocks_ref):
    rows = share_ref.shape[0]
    line = lax.broadcasted_iota(jnp.int32, (rows, rows), 0)
    lane = lax.broadcasted_iota(jnp.int32, (rows, rows), 1)
    alpha = share_ref[:, :rows]
    mean = share_ref[0:1, 4 * rows - 1 : 4 * rows]
    gram = share_ref[:, rows : 2 * rows] - mm_t(alpha, alpha)
    beta, inverse = factor(gram)
    next_ref[...] = mm(inverse, result_ref[...] - mm(alpha, basis_ref[...]))
    blocks_ref[0] = share_ref[:, 2 * rows : 3 * rows]
    blocks_ref[1] = jnp.where(lane > line, 0.0, share_ref[:, 3 * rows :])
    blocks_ref[2] = alpha + jnp.where(line == lane, mean, 0.0)
    blocks_ref[3] = beta


def call(kernel, out_shape, args, smem=0, hbm=0, scratch=(), room=8):
    args = [pltpu.with_memory_space_constraint(a, pltpu.HBM) if j < smem + hbm else a for j, a in enumerate(args)]
    outs = in_vmem if not isinstance(out_shape, tuple) else (in_vmem,) * len(out_shape)
    return pl.pallas_call(
        kernel,
        out_shape=out_shape,
        in_specs=[in_smem] * smem + [in_hbm] * hbm + [in_vmem] * (len(args) - smem - hbm),
        out_specs=outs,
        scratch_shapes=list(scratch),
        compiler_params=pltpu.CompilerParams(vmem_limit_bytes=room * 1024 * 1024),
        cost_estimate=pl.CostEstimate(flops=1, bytes_accessed=1, transcendentals=0),
    )(*args)


def body(probes, diagonal, forward_tiles, tile_columns):
    forward = forward_tiles[0]
    rows, order = probes.shape
    devices = lax.axis_size("col")

    def swapped(block, bits=1):
        return lax.ppermute(block, "col", [(i ^ bits, i) for i in range(devices)])

    def from_chips(block, *chips):
        hops = [chips[i & 1] for i in range(devices)]
        route = [((i + 2 * hops[i]) % devices, i) for i in range(devices) if hops[i] is not None]
        return lax.ppermute(block, "col", route)

    def whole(sums):
        bits = 2
        while bits < devices:
            sums = sums + swapped(sums, bits)
            bits *= 2
        return sums

    def apply(bundle, keep, near_call):
        top = bundle.shape[0] - keep.shape[0]
        partner = swapped(bundle)
        own, its = bundle[:size], partner[:size]
        payload = bundle[size:top] + partner[size:top]
        pair = jnp.concatenate([jnp.where(lower, own, its), jnp.where(lower, its, own), payload])
        ahead = keep + partner[top:]
        near_ahead = jnp.concatenate([ahead[: 2 * size], payload])
        third_ahead = jnp.where(both_lower, pair[: 2 * size], ahead[2 * size : 4 * size])
        third_ahead = jnp.concatenate([third_ahead, payload])
        fourth_ahead = jnp.concatenate([jnp.where(lower, pair[:size], ahead[4 * size : 5 * size]), payload])
        near = from_chips(pair, 1, 2)
        near_back = from_chips(near_ahead, -1, -2)
        third = from_chips(third_ahead, 3, -3)
        fourth = from_chips(fourth_ahead, 4, -4)
        bundle, _, _ = lax.optimization_barrier((bundle, near_ahead, third_ahead))
        inner, turned = near_call(bundle)
        near, near_back, third, fourth, inner, turned = lax.optimization_barrier(
            (near, near_back, third, fourth, inner, turned)
        )
        mine = jnp.concatenate([near[: 2 * size], third[: 2 * size], fourth[:size]])
        if devices == 16:
            sums = near[2 * size :] + near_back[2 * size :] + third[2 * size :]
            sums = sums + jnp.where(lower[: top - size], payload + fourth[size:], 0.0)
        else:
            sums = jnp.where(lower[: top - size], whole(payload), 0.0)
        first = near_back[:size] + jnp.where(lower, 0.0, third[:size] + fourth[:size])
        second = near_back[size : 2 * size] + jnp.where(lower, 0.0, third[size : 2 * size] + ahead[5 * size :])
        other = jnp.concatenate([jnp.where(lower, second, first), sums])
        mine, other = lax.optimization_barrier((mine, other))
        theirs, other = swapped(mine), swapped(other)
        total = jnp.where(lower, first, second) + other[:size]
        return inner, total, sums + other[size:], (pair, mine, theirs), turned

    tiles = forward.shape[0]
    size = rows * order // (PAD * SIDE)
    slots = struct(SLOTS * size, PAD, SIDE)
    bundles = [struct(size + notes + SLOTS * size, PAD, SIDE) for notes in (1, 2)]
    products = pltpu.VMEM((tiles, rows, order), jnp.float32)
    split = pltpu.VMEM(forward.shape, jnp.bfloat16)
    split_diagonal = pltpu.VMEM(diagonal.shape, jnp.bfloat16)
    start, core, keep, high, low = call(
        begin_kernel,
        (bundles[0], pltpu.VMEM((size, PAD, SIDE), jnp.int32), slots, split, split),
        (tile_columns, probes, diagonal, forward),
        smem=1,
        hbm=3,
        room=12,
        scratch=(
            pltpu.VMEM(probes.shape, jnp.int32),
            pltpu.VMEM((order // SIDE, SIDE, SIDE), jnp.float32),
            pltpu.VMEM(forward.shape, jnp.float32),
            products,
            pltpu.SemaphoreType.DMA((tiles + 1 + order // SIDE,)),
        ),
    )
    lower = core == 0
    both_lower = jnp.concatenate([lower, lower])

    def first_near(bundle):
        made = call(
            first_near_kernel,
            (struct(rows, order), split_diagonal, split_diagonal, split, split),
            (bundle, diagonal, high, low),
        )
        return made[0], made[1:]

    inner, total, start_sums, met, turned = apply(start, keep, first_near)
    diagonal_high, diagonal_low, *turned = turned
    ready = pltpu.VMEM((tiles, 2 * rows, order), jnp.bfloat16)
    message, keep = call(
        functools.partial(first_kernel, devices),
        (bundles[1], slots),
        (tile_columns, start, inner, total, start_sums, high, low, *met, *turned),
        smem=1,
        scratch=(products, ready),
    )

    def second_near(bundle):
        inner = call(second_near_kernel, struct(rows, order), (bundle, diagonal_high, diagonal_low))
        ahead = call(
            functools.partial(root_kernel, devices),
            (struct(rows, rows), struct(rows, 2 * order)),
            (start_sums, start, bundle),
        )
        return inner, ahead

    inner, total, sums, met, (root, lines) = apply(message, keep, second_near)
    basis, result, share = call(
        functools.partial(second_kernel, devices),
        (struct(rows, order), struct(rows, order), struct(rows, SIDE)),
        (tile_columns, start, message, inner, total, root, lines, start_sums, sums, *met, *turned),
        smem=1,
        scratch=(ready,),
    )
    low = 1
    strides = []
    while low < devices:
        strides.append((low, (1, 2, 3) if 4 * low <= devices else (1,)))
        low *= 4 if 4 * low <= devices else 2
    for bits, steps in reversed(strides):
        got = [swapped(share, bits * j) for j in steps]
        share = share + got[0] if len(got) == 1 else (share + got[0]) + (got[1] + got[2])
    outs = (jax.ShapeDtypeStruct((rows, order), jnp.float32), jax.ShapeDtypeStruct((4, rows, rows), jnp.float32))
    return call(last_kernel, outs, (share, basis, result))


def solution(mesh):
    placed = (
        P(None, ("groups", "col")),
        P(("groups", "col"), None),
        P(("groups", "col"), None, None, None),
        P(("groups", "col"), None),
    )
    return jax.shard_map(
        body,
        mesh=mesh,
        in_specs=placed,
        out_specs=(P(None, ("groups", "col")), P("groups", None, None)),
        check_vma=False,
    )
```
